512 devices in a mesh: seq: 32 (over z, x_hi), chan: 16 (over x_lo, y, core).
Axes of the slice: x: 4 (x_hi: 2, x_lo: 2; x = x_hi * 2 + x_lo), y: 4, z: 16, core: 2. Of those that a mesh axis runs over, the one named last changes fastest.
Arguments:
- query: bfloat16 [32, 16, 8192], P('chan', None, 'seq'), may hold values from -6 to 6
- key_in: bfloat16 [32, 16, 8192], P('chan', None, 'seq'), may hold values from -6 to 6
- value: bfloat16 [32, 16, 8192], P('chan', None, 'seq'), may hold values from -6 to 6
- grad_out: bfloat16 [32, 16, 8192], P('chan', None, 'seq'), may hold values from -6 to 6
- filters: float32 [16, 8192], P(None, 'seq'), may hold values from -2 to 2
- skip: float32 [32, 16], P('chan'), may hold values from 0.5 to 1.5
Outputs:
- query_grad: bfloat16 [32, 16, 8192], P('chan', None, 'seq')
- key_grad: bfloat16 [32, 16, 8192], P('chan', None, 'seq')
- value_grad: bfloat16 [32, 16, 8192], P('chan', None, 'seq')
- filter_grad: float32 [16, 8192], P('chan', 'seq')
The draws below stay inside these ranges and needn't reach their ends.
All inputs are finite; a program needn't handle non-finite values.
Results may differ from the reference program's by a relative error of at most 0.0028.
Values sent between devices are 32-bit elements; how exact they have to be, the bound alone decides.
No kernel may reach another device: no remote copies, remote signals or barrier semaphores. Data moves between devices by JAX's collectives and lax.ppermute only.
A program may use at most 64 MiB of HBM per device.

```python
import math
import jax
import jax.numpy as jnp
from jax import lax

GROUP_CH = 32
GROUPS = 16
LEN = 8192


def draw_filters(key, part):
    key = jax.random.fold_in(key, 7)
    rate_key, tap_key = jax.random.split(key)
    lower = 1.0 / LEN
    upper = 1.0 / 30.0
    rates = jnp.exp(jax.random.uniform(rate_key, (GROUPS, 1), jnp.float32, jnp.log(lower), jnp.log(upper)))
    lags = jnp.arange(LEN, dtype=jnp.float32)[None, :]
    amplitude = jnp.sqrt((1.0 - jnp.exp(-2.0 * rates)) / (1.0 - jnp.exp(-2.0 * rates * LEN)))
    noise = jax.random.truncated_normal(tap_key, -4.0, 4.0, (GROUPS, LEN), jnp.float32)
    return noise * amplitude * jnp.exp(-rates * lags)


def strengthened(array, stream_key, source, target, shards_of, factor):
    owner, partner = [(jnp.arange(array.shape[dim]) // (array.shape[dim] // shards_of)).reshape([-1 if axis == dim else 1 for axis in range(array.ndim)]) for dim in (source, target)]
    chosen = jax.random.permutation(stream_key, shards_of)[partner]
    strong = (owner == chosen) | (owner == (partner + shards_of // 2) % shards_of)
    return jnp.where(strong, factor * array, array)


def block_scale(own_key, extent, cuts, low, high):
    def one(position, shards_of):
        draws = jax.random.uniform(jax.random.fold_in(jax.random.fold_in(own_key, 6), position), (shards_of,), jnp.float32, low / len(cuts), high / len(cuts))
        return jnp.repeat(jnp.exp(draws), extent[position] // shards_of).reshape((-1,) + (1,) * (len(extent) - position - 1))

    gain = one(*cuts[0])
    for cut in cuts[1:]:
        gain = gain * one(*cut)
    return gain


def centred(rng, shape, spread, limit, shards=(), kind=jnp.bfloat16):
    values = spread * jax.random.normal(rng, shape, jnp.float32)
    if shards:
        values = values * block_scale(rng, shape, shards, -0.22, 0.18)
    return jnp.clip(values, -limit, limit).astype(kind)


def bell_draw_with(stream_key, dims, scale, limit, cuts, heavy, kind=jnp.bfloat16):
    drawn = scale * jax.random.normal(stream_key, dims, jnp.float32)
    if cuts:
        drawn = drawn * block_scale(stream_key, dims, cuts, -0.22, 0.18)
    return jnp.clip(strengthened(drawn, jax.random.fold_in(stream_key, 3), *heavy), -limit, limit).astype(kind)


def setup_inputs(seed: int = 0) -> dict:
    streams_of = jax.random.split(jax.random.key(seed), 7)
    return {
        "query": centred(streams_of[0], (GROUP_CH, GROUPS, LEN), 1.0, 6.0, ((0, 16), (2, 32))),
        "key_in": centred(streams_of[1], (GROUP_CH, GROUPS, LEN), 1.0, 6.0, ((0, 16), (2, 32))),
        "value": centred(streams_of[2], (GROUP_CH, GROUPS, LEN), 1.0, 6.0, ((0, 16), (2, 32))),
        "grad_out": bell_draw_with(streams_of[3], (GROUP_CH, GROUPS, LEN), 1.0, 6.0, ((0, 16), (2, 32)), (0, 1, 16, 2.0)),
        "filters": draw_filters(jax.random.fold_in(streams_of[6], 71), 0),
        "skip": jnp.clip(0.5 + 1.0 * jax.random.uniform(streams_of[5], (GROUP_CH, GROUPS), jnp.float32) ** block_scale(streams_of[5], (GROUP_CH, GROUPS), ((0, 16),), -0.2, 0.2), 0.5, 1.5),
    }


def reference(query, key_in, value, grad_out, filters, skip):
    full_length = 2 * LEN
    filter_spec = jnp.fft.rfft(filters.astype(jnp.float32), n=full_length)
    spec_width = full_length // 2 + 1

    def per_slot(running, inputs):
        query_f = inputs[0].astype(jnp.float32)
        key_f = inputs[1].astype(jnp.float32)
        value_f = inputs[2].astype(jnp.float32)
        cotangent = inputs[3].astype(jnp.float32)
        skip_gain = inputs[4][:, None]
        gated = query_f * key_f
        signal = cotangent * value_f
        gated_spec = jnp.fft.rfft(gated, n=full_length)
        signal_spec = jnp.fft.rfft(signal, n=full_length)
        conv = jnp.fft.irfft(filter_spec * gated_spec, n=full_length)[:, :LEN]
        corr = jnp.fft.irfft(jnp.conj(filter_spec) * signal_spec, n=full_length)[:, :LEN]
        out_field = conv + skip_gain * gated
        adjoint = corr + skip_gain * signal
        cross = jnp.conj(gated_spec) * signal_spec
        running = (running[0] + jnp.real(cross), running[1] + jnp.imag(cross))
        grads = ((adjoint * key_f).astype(jnp.bfloat16), (adjoint * query_f).astype(jnp.bfloat16), (cotangent * out_field).astype(jnp.bfloat16))
        return (running, grads)
    empty_sum = jnp.zeros((GROUPS, spec_width), jnp.float32)
    sums, grads = lax.scan(per_slot, (empty_sum, empty_sum), (query, key_in, value, grad_out, skip))
    lagged = jnp.fft.irfft(sums[0] + 1j * sums[1], n=full_length)[:, :LEN]
    filter_grad = (lagged * (1.0 / math.sqrt(GROUP_CH * LEN))).astype(jnp.float32)
    return (grads[0], grads[1], grads[2], filter_grad)
```

```python
import functools
import math

import jax
import jax.numpy as jnp
import ml_dtypes
import numpy as np
from jax import lax
from jax.experimental import pallas as pl
from jax.experimental.pallas import tpu as pltpu
from jax.sharding import PartitionSpec as P

LANES = 128
VMEM = pl.BlockSpec(memory_space=pltpu.VMEM)
LIMIT = 24 * 1024 * 1024


def split_table(table):
    high = table.astype(ml_dtypes.bfloat16)
    low = (table - high.astype(np.float64)).astype(ml_dtypes.bfloat16)
    return high, low


def half_rows(side):
    return -(-(side // 2 + 1) // 8) * 8


def fourier_tables(side, parts):
    used = side // 2 + 1
    rows = half_rows(side)
    per_block = side // 2 // parts
    order = np.arange(side // 2).reshape(parts, per_block).T.reshape(-1)
    coarse = np.arange(used)
    angle = 2.0 * math.pi / side * (coarse[:, None] * order[None, :] % side)
    first = np.zeros((2, rows, side // 2))
    first[0, :used] = np.cos(angle)
    first[1, :used] = -np.sin(angle)
    first = first.reshape(2 * rows, side // 2)
    weight = np.full((used,), 2.0)
    weight[0] = weight[-1] = 1.0
    last = np.zeros((side // 2, 2, rows))
    last[:, 0, :used] = (weight[:, None] * np.cos(angle)).T / side**2
    last[:, 1, :used] = (weight[:, None] * np.sin(angle)).T / side**2
    last = last.reshape(side // 2, 2 * rows)
    turn = 2.0 * math.pi / side**2 * (coarse[:, None] * np.arange(side)[None, :])
    twist = np.zeros((2, rows, side), np.float32)
    twist[0, :used] = np.cos(turn)
    twist[1, :used] = -np.sin(turn)
    fine = 2.0 * math.pi / side * (np.arange(side)[:, None] * np.arange(side)[None, :] % side)
    fine_re, fine_im = np.cos(fine), -np.sin(fine)
    mix = np.block([[fine_re, fine_im], [-fine_im, fine_re]])
    first_high, first_low = split_table(first)
    first = np.concatenate([first_high, first_high, first_low], axis=1)
    return first, twist, *split_table(mix), *split_table(last)


def halves(values):
    high = values.astype(jnp.bfloat16)
    low = (values - high.astype(jnp.float32)).astype(jnp.bfloat16)
    return high, low


def matmul(left, right):
    return jnp.dot(left, right, preferred_element_type=jnp.float32)


def gate_kernel(query, key_in, value, grad_out, filters, sent):
    slots, groups, length = query.shape
    per_row = length // LANES
    pieces = 3 * per_row
    taps = filters[...]
    for slot in range(slots):
        gated = query[slot].astype(jnp.float32) * key_in[slot].astype(jnp.float32)
        signal = grad_out[slot].astype(jnp.float32) * value[slot].astype(jnp.float32)
        base = pieces * groups * slot
        for which, rows in enumerate((gated, signal, taps)):
            for part in range(per_row):
                place = pl.ds(base + which * per_row + part, groups, stride=pieces)
                sent[place, :] = rows[:, part * LANES : (part + 1) * LANES]


def spectral_kernel(side, parts, got, first, twist, mix_high, mix_low, last_high, last_low, sent):
    rows = half_rows(side)
    per_row = side // 2 // parts
    pieces = 3 * per_row

    def one(which):
        return jnp.concatenate(
            [got[pl.ds(which * per_row + part, parts, stride=pieces), :] for part in range(per_row)], axis=0
        )

    high, low = halves(jnp.concatenate([one(which) for which in range(3)], axis=1))
    coarse = matmul(first[...], jnp.concatenate([high, low, high], axis=0))
    turn_re, turn_im = twist[0], twist[1]

    def turned(real, imag):
        return real * turn_re - imag * turn_im, real * turn_im + imag * turn_re

    def mixed(values):
        high, low = halves(values)
        return matmul(high, mix_high[...]) + (matmul(low, mix_high[...]) + matmul(high, mix_low[...]))

    stacked = []
    for which in range(3):
        lanes = slice(which * side, (which + 1) * side)
        stacked.append(jnp.concatenate(turned(coarse[:rows, lanes], coarse[rows:, lanes]), axis=1))
    spectra = mixed(jnp.concatenate(stacked, axis=0))
    (gated_re, gated_im), (signal_re, signal_im), (taps_re, taps_im) = [
        (spectra[which * rows : (which + 1) * rows, :side], spectra[which * rows : (which + 1) * rows, side:])
        for which in range(3)
    ]
    conv = (taps_re * gated_re - taps_im * gated_im, -(taps_re * gated_im + taps_im * gated_re))
    corr = (taps_re * signal_re + taps_im * signal_im, taps_im * signal_re - taps_re * signal_im)
    cross = (gated_re * signal_re + gated_im * signal_im, gated_im * signal_re - gated_re * signal_im)
    products = mixed(jnp.concatenate([jnp.concatenate(pair, axis=1) for pair in (conv, corr, cross)], axis=0))
    turned_re, turned_im = [], []
    for which in range(3):
        block = products[which * rows : (which + 1) * rows]
        real, imag = turned(block[:, :side], block[:, side:])
        turned_re.append(real)
        turned_im.append(imag)
    high, low = halves(
        jnp.concatenate([jnp.concatenate(turned_re, axis=1), jnp.concatenate(turned_im, axis=1)], axis=0)
    )
    result = matmul(last_high[...], high) + (matmul(last_high[...], low) + matmul(last_low[...], high))
    for which in range(3):
        for part in range(per_row):
            sent[pl.ds(which * per_row + part, parts, stride=pieces), :] = result[
                part * parts : (part + 1) * parts, which * side : (which + 1) * side
            ]


def share_kernel(slots, groups, got, sent):
    per_row = sent.shape[0] // groups
    pieces = 3 * per_row
    for part in range(per_row):
        total = got[pl.ds(2 * per_row + part, groups, stride=pieces), :]
        for slot in range(1, slots):
            total += got[pl.ds(slot * pieces * groups + 2 * per_row + part, groups, stride=pieces), :]
        sent[pl.ds(part, groups, stride=per_row), :] = total


def grads_kernel(got, query, key_in, value, grad_out, skip, query_grad, key_grad, value_grad):
    slots, groups, length = query.shape
    per_row = length // LANES
    pieces = 3 * per_row
    shape = (groups, groups)
    diagonal = lax.broadcasted_iota(jnp.int32, shape, 0) == lax.broadcasted_iota(jnp.int32, shape, 1)
    for slot in range(slots):
        gains = jnp.broadcast_to(skip[slot : slot + 1, :], shape)
        gain = jnp.sum(jnp.where(diagonal, gains, 0.0), axis=1, keepdims=True)
        base = slot * pieces * groups
        for part in range(per_row):
            lanes = slice(part * LANES, (part + 1) * LANES)
            conv = got[pl.ds(base + part, groups, stride=pieces), :]
            corr = got[pl.ds(base + per_row + part, groups, stride=pieces), :]
            query_f = query[slot, :, lanes].astype(jnp.float32)
            key_f = key_in[slot, :, lanes].astype(jnp.float32)
            cotangent = grad_out[slot, :, lanes].astype(jnp.float32)
            out_field = conv + gain * (query_f * key_f)
            adjoint = corr + gain * (cotangent * value[slot, :, lanes].astype(jnp.float32))
            query_grad[slot, :, lanes] = (adjoint * key_f).astype(jnp.bfloat16)
            key_grad[slot, :, lanes] = (adjoint * query_f).astype(jnp.bfloat16)
            value_grad[slot, :, lanes] = (cotangent * out_field).astype(jnp.bfloat16)


def filter_kernel(scale, got, filter_grad):
    per_row = filter_grad.shape[1] // LANES
    senders = got.shape[0] // per_row
    for part in range(per_row):
        rows = got[pl.ds(part, senders, stride=per_row), :]
        filter_grad[:, part * LANES : (part + 1) * LANES] = scale * jnp.sum(rows, axis=0, keepdims=True)


def on_device(kernel, shapes, count):
    outs = jax.tree.map(lambda shape: VMEM, shapes)
    return pl.pallas_call(
        kernel,
        out_shape=shapes,
        in_specs=[VMEM] * count,
        out_specs=outs,
        compiler_params=pltpu.CompilerParams(vmem_limit_bytes=LIMIT),
    )


def exchange(rows, axis, count):
    blocks = rows.reshape(count, 1, rows.size // count)
    return lax.all_to_all(blocks, axis, 0, 0, tiled=True).reshape(rows.shape)


def local(query, key_in, value, grad_out, filters, skip):
    parts = lax.axis_size("seq")
    chans = lax.axis_size("chan")
    slots, groups, length = query.shape
    total = parts * length
    side = math.isqrt(2 * total)
    pieces = 3 * length // LANES
    packed = jax.ShapeDtypeStruct((parts * pieces, LANES), jnp.float32)
    sent = on_device(gate_kernel, packed, 5)(query, key_in, value, grad_out, filters)
    got = exchange(sent, "seq", parts)
    tables = fourier_tables(side, parts)
    spectral = functools.partial(spectral_kernel, side, parts)
    sent = on_device(spectral, packed, 1 + len(tables))(got, *tables)
    got = exchange(sent, "seq", parts)
    shared = jax.ShapeDtypeStruct((groups * length // LANES, LANES), jnp.float32)
    lagged = on_device(functools.partial(share_kernel, slots, groups), shared, 1)(got)
    lagged = exchange(lagged, "chan", chans)
    grad = jax.ShapeDtypeStruct(query.shape, jnp.bfloat16)
    grads = on_device(grads_kernel, (grad, grad, grad), 6)(got, query, key_in, value, grad_out, skip)
    scale = 1.0 / math.sqrt(slots * chans * total)
    row = jax.ShapeDtypeStruct((1, length), jnp.float32)
    filter_grad = on_device(functools.partial(filter_kernel, scale), row, 1)(lagged)
    return (*grads, filter_grad)


def solution(mesh):
    spread = P("chan", None, "seq")
    return jax.shard_map(
        local,
        mesh=mesh,
        in_specs=(spread, spread, spread, spread, P(None, "seq"), P("chan", None)),
        out_specs=(spread, spread, spread, P("chan", "seq")),
        check_vma=False,
    )
```

```python
import functools
import math

import jax
import jax.numpy as jnp
import ml_dtypes
import numpy as np
from jax import lax
from jax.experimental import pallas as pl
from jax.experimental.pallas import tpu as pltpu
from jax.sharding import PartitionSpec as P

LANES = 128
VMEM = pl.BlockSpec(memory_space=pltpu.VMEM)
HBM = pl.BlockSpec(memory_space=pltpu.HBM)
LIMIT = 16 * 1024 * 1024


def split_table(table):
    high = table.astype(ml_dtypes.bfloat16)
    low = (table - high.astype(np.float64)).astype(ml_dtypes.bfloat16)
    return high, low


def half_rows(side):
    return -(-(side // 2 + 1) // 8) * 8


def fourier_tables(side, parts):
    used = side // 2 + 1
    rows = half_rows(side)
    per_block = side // 2 // parts
    order = np.arange(side // 2).reshape(parts, per_block).T.reshape(-1)
    coarse = np.arange(used)
    angle = 2.0 * math.pi / side * (coarse[:, None] * order[None, :] % side)
    first = np.zeros((2, rows, side // 2))
    first[0, :used] = np.cos(angle)
    first[1, :used] = -np.sin(angle)
    first = first.reshape(2 * rows, side // 2)
    weight = np.full((used,), 2.0)
    weight[0] = weight[-1] = 1.0
    last = np.zeros((side // 2, 2, rows))
    last[:, 0, :used] = (weight[:, None] * np.cos(angle)).T / side**2
    last[:, 1, :used] = (weight[:, None] * np.sin(angle)).T / side**2
    last = last.reshape(side // 2, 2 * rows)
    turn = 2.0 * math.pi / side**2 * (coarse[:, None] * np.arange(side)[None, :])
    twist = np.zeros((2, rows, side), np.float32)
    twist[0, :used] = np.cos(turn)
    twist[1, :used] = -np.sin(turn)
    fine = 2.0 * math.pi / side * (np.arange(side)[:, None] * np.arange(side)[None, :] % side)
    fine_re, fine_im = np.cos(fine), -np.sin(fine)
    mix = np.block([[fine_re, fine_im], [-fine_im, fine_re]])
    first_high, first_low = split_table(first)
    first = np.concatenate([first_high, first_high, first_low], axis=1)
    blocks = [*split_table(mix), first, *split_table(last)]
    wide = max(block.shape[1] for block in blocks)
    stacked = [np.pad(block, ((0, 0), (0, wide - block.shape[1]))) for block in blocks]
    return np.concatenate(stacked, axis=0), twist


def table_slices(side):
    rows = half_rows(side)
    sizes = ((2 * side, 2 * side),) * 2 + ((2 * rows, 3 * side // 2),) + ((side // 2, 2 * rows),) * 2
    starts = np.cumsum([0] + [size[0] for size in sizes])
    return [
        (slice(int(start), int(start) + height), slice(0, width))
        for start, (height, width) in zip(starts, sizes)
    ]


def halves(values):
    high = values.astype(jnp.bfloat16)
    low = (values - high.astype(jnp.float32)).astype(jnp.bfloat16)
    return high, low


def matmul(left, right):
    return jnp.dot(left, right, preferred_element_type=jnp.float32)


def gate_kernel(
    query, key_in, value, grad_out, filters, skip, tables, twist,
    sent, inputs, gains, tables_held, twist_held, taps, sems,
):
    slots, groups, length = query.shape
    per_row = length // LANES
    pieces = 3 * per_row
    pairs = [(source, inputs.at[place]) for place, source in enumerate((query, key_in, grad_out, value))]
    pairs += [(filters, taps), (skip, gains), (tables, tables_held), (twist, twist_held)]
    copies = [pltpu.make_async_copy(*pair, sems.at[place]) for place, pair in enumerate(pairs)]
    for copy in copies:
        copy.start()
    for copy in copies[:5]:
        copy.wait()
    for slot in range(slots):
        query_f, key_f, cotangent, value_f = [inputs[place, slot].astype(jnp.float32) for place in range(4)]
        base = pieces * groups * slot
        for which, rows in enumerate((query_f * key_f, cotangent * value_f, taps[...])):
            for part in range(per_row):
                place = pl.ds(base + which * per_row + part, groups, stride=pieces)
                sent[place, :] = rows[:, part * LANES : (part + 1) * LANES]
    for copy in copies[5:]:
        copy.wait()


def spectral_kernel(side, parts, got, tables, twist, sent):
    mix_high, mix_low, first, last_high, last_low = [tables[place] for place in table_slices(side)]
    rows = half_rows(side)
    per_row = side // 2 // parts
    pieces = 3 * per_row

    def one(which):
        return jnp.concatenate(
            [got[pl.ds(which * per_row + part, parts, stride=pieces), :] for part in range(per_row)], axis=0
        )

    high, low = halves(jnp.concatenate([one(which) for which in range(3)], axis=1))
    coarse = matmul(first, jnp.concatenate([high, low, high], axis=0))
    turn_re, turn_im = twist[0], twist[1]

    def turned(real, imag):
        return real * turn_re - imag * turn_im, real * turn_im + imag * turn_re

    def mixed(values):
        high, low = halves(values)
        return matmul(high, mix_high) + (matmul(low, mix_high) + matmul(high, mix_low))

    stacked = []
    for which in range(3):
        lanes = slice(which * side, (which + 1) * side)
        stacked.append(jnp.concatenate(turned(coarse[:rows, lanes], coarse[rows:, lanes]), axis=1))
    spectra = mixed(jnp.concatenate(stacked, axis=0))
    (gated_re, gated_im), (signal_re, signal_im), (taps_re, taps_im) = [
        (spectra[which * rows : (which + 1) * rows, :side], spectra[which * rows : (which + 1) * rows, side:])
        for which in range(3)
    ]
    conv = (taps_re * gated_re - taps_im * gated_im, -(taps_re * gated_im + taps_im * gated_re))
    corr = (taps_re * signal_re + taps_im * signal_im, taps_im * signal_re - taps_re * signal_im)
    cross = (gated_re * signal_re + gated_im * signal_im, gated_im * signal_re - gated_re * signal_im)
    products = mixed(jnp.concatenate([jnp.concatenate(pair, axis=1) for pair in (conv, corr, cross)], axis=0))
    turned_re, turned_im = [], []
    for which in range(3):
        block = products[which * rows : (which + 1) * rows]
        real, imag = turned(block[:, :side], block[:, side:])
        turned_re.append(real)
        turned_im.append(imag)
    high, low = halves(
        jnp.concatenate([jnp.concatenate(turned_re, axis=1), jnp.concatenate(turned_im, axis=1)], axis=0)
    )
    result = matmul(last_high, high) + (matmul(last_high, low) + matmul(last_low, high))
    for which in range(3):
        for part in range(per_row):
            sent[pl.ds(which * per_row + part, parts, stride=pieces), :] = result[
                part * parts : (part + 1) * parts, which * side : (which + 1) * side
            ]


def share_kernel(slots, groups, got, sent):
    per_row = sent.shape[0] // groups
    pieces = 3 * per_row
    for part in range(per_row):
        total = got[pl.ds(2 * per_row + part, groups, stride=pieces), :]
        for slot in range(1, slots):
            total += got[pl.ds(slot * pieces * groups + 2 * per_row + part, groups, stride=pieces), :]
        sent[pl.ds(part, groups, stride=per_row), :] = total


def grads_kernel(got, inputs, skip, query_grad, key_grad, value_grad):
    _, slots, groups, length = inputs.shape
    per_row = length // LANES
    pieces = 3 * per_row
    shape = (groups, groups)
    diagonal = lax.broadcasted_iota(jnp.int32, shape, 0) == lax.broadcasted_iota(jnp.int32, shape, 1)
    for slot in range(slots):
        gains = jnp.broadcast_to(skip[slot : slot + 1, :], shape)
        gain = jnp.sum(jnp.where(diagonal, gains, 0.0), axis=1, keepdims=True)
        base = slot * pieces * groups
        for part in range(per_row):
            lanes = slice(part * LANES, (part + 1) * LANES)
            conv = got[pl.ds(base + part, groups, stride=pieces), :]
            corr = got[pl.ds(base + per_row + part, groups, stride=pieces), :]
            query_f, key_f, cotangent, value_f = [
                inputs[place, slot, :, lanes].astype(jnp.float32) for place in range(4)
            ]
            out_field = conv + gain * (query_f * key_f)
            adjoint = corr + gain * (cotangent * value_f)
            query_grad[slot, :, lanes] = (adjoint * key_f).astype(jnp.bfloat16)
            key_grad[slot, :, lanes] = (adjoint * query_f).astype(jnp.bfloat16)
            value_grad[slot, :, lanes] = (cotangent * out_field).astype(jnp.bfloat16)


def filter_kernel(scale, got, filter_grad):
    per_row = filter_grad.shape[1] // LANES
    senders = got.shape[0] // per_row
    for part in range(per_row):
        rows = got[pl.ds(part, senders, stride=per_row), :]
        filter_grad[:, part * LANES : (part + 1) * LANES] = scale * jnp.sum(rows, axis=0, keepdims=True)


def on_device(kernel, shapes, count, space=VMEM, scratch=()):
    outs = jax.tree.map(lambda shape: VMEM, shapes)
    return pl.pallas_call(
        kernel,
        out_shape=shapes,
        in_specs=[space] * count,
        out_specs=outs,
        scratch_shapes=scratch,
        compiler_params=pltpu.CompilerParams(vmem_limit_bytes=LIMIT),
    )


def in_hbm(array):
    return pltpu.with_memory_space_constraint(jnp.asarray(array), pltpu.HBM)


def exchange(rows, axis, count):
    blocks = rows.reshape(count, 1, rows.size // count)
    return lax.all_to_all(blocks, axis, 0, 0, tiled=True).reshape(rows.shape)


def local(query, key_in, value, grad_out, filters, skip):
    parts = lax.axis_size("seq")
    chans = lax.axis_size("chan")
    slots, groups, length = query.shape
    total = parts * length
    side = math.isqrt(2 * total)
    pieces = 3 * length // LANES
    packed = jax.ShapeDtypeStruct((parts * pieces, LANES), jnp.float32)
    tables, twist = fourier_tables(side, parts)
    shapes = (
        packed,
        jax.ShapeDtypeStruct((4, *query.shape), query.dtype),
        *[jax.ShapeDtypeStruct(array.shape, array.dtype) for array in (skip, tables, twist)],
    )
    scratch = [pltpu.VMEM(filters.shape, jnp.float32), pltpu.SemaphoreType.DMA((8,))]
    sent, inputs, gains, tables, twist = on_device(gate_kernel, shapes, 8, HBM, scratch)(
        *[in_hbm(array) for array in (query, key_in, value, grad_out, filters, skip, tables, twist)]
    )
    got = exchange(sent, "seq", parts)
    spectral = functools.partial(spectral_kernel, side, parts)
    sent = on_device(spectral, packed, 3)(got, tables, twist)
    got = exchange(sent, "seq", parts)
    shared = jax.ShapeDtypeStruct((groups * length // LANES, LANES), jnp.float32)
    lagged = on_device(functools.partial(share_kernel, slots, groups), shared, 1)(got)
    lagged = exchange(lagged, "chan", chans)
    grad = jax.ShapeDtypeStruct(query.shape, jnp.bfloat16)
    grads = on_device(grads_kernel, (grad, grad, grad), 3)(got, inputs, gains)
    scale = 1.0 / math.sqrt(slots * chans * total)
    row = jax.ShapeDtypeStruct((1, length), jnp.float32)
    filter_grad = on_device(functools.partial(filter_kernel, scale), row, 1)(lagged)
    return (*grads, filter_grad)


def solution(mesh):
    spread = P("chan", None, "seq")
    return jax.shard_map(
        local,
        mesh=mesh,
        in_specs=(spread, spread, spread, spread, P(None, "seq"), P("chan", None)),
        out_specs=(spread, spread, spread, P("chan", "seq")),
        check_vma=False,
    )
```

```python
import functools
import math

import jax
import jax.numpy as jnp
import ml_dtypes
import numpy as np
from jax import lax
from jax.experimental import pallas as pl
from jax.experimental.pallas import tpu as pltpu
from jax.sharding import PartitionSpec as P

LANES = 128
VMEM = pl.BlockSpec(memory_space=pltpu.VMEM)
HBM = pl.BlockSpec(memory_space=pltpu.HBM)
LIMIT = 16 * 1024 * 1024


def split_table(table):
    high = table.astype(ml_dtypes.bfloat16)
    low = (table - high.astype(np.float64)).astype(ml_dtypes.bfloat16)
    return high, low


def half_rows(side):
    return -(-(side // 2 + 1) // 8) * 8


def fourier_tables(side, parts):
    used = side // 2 + 1
    rows = half_rows(side)
    per_block = side // 2 // parts
    order = np.arange(side // 2).reshape(parts, per_block).T.reshape(-1)
    coarse = np.arange(used)
    angle = 2.0 * math.pi / side * (coarse[:, None] * order[None, :] % side)
    first = np.zeros((2, rows, side // 2))
    first[0, :used] = np.cos(angle)
    first[1, :used] = -np.sin(angle)
    first = first.reshape(2 * rows, side // 2)
    weight = np.full((used,), 2.0)
    weight[0] = weight[-1] = 1.0
    last = np.zeros((side // 2, 2, rows))
    last[:, 0, :used] = (weight[:, None] * np.cos(angle)).T / side**2
    last[:, 1, :used] = (weight[:, None] * np.sin(angle)).T / side**2
    last = last.reshape(side // 2, 2 * rows)
    turn = 2.0 * math.pi / side**2 * (coarse[:, None] * np.arange(side)[None, :])
    twist = np.zeros((2, rows, side), np.float32)
    twist[0, :used] = np.cos(turn)
    twist[1, :used] = -np.sin(turn)
    fine = 2.0 * math.pi / side * (np.arange(side)[:, None] * np.arange(side)[None, :] % side)
    fine_re, fine_im = np.cos(fine), -np.sin(fine)
    mix = np.block([[fine_re, fine_im], [-fine_im, fine_re]])
    first_high, first_low = split_table(first)
    first = np.concatenate([first_high, first_high, first_low], axis=1)
    blocks = [*split_table(mix), first, *split_table(last)]
    wide = max(block.shape[1] for block in blocks)
    stacked = [np.pad(block, ((0, 0), (0, wide - block.shape[1]))) for block in blocks]
    return np.concatenate(stacked, axis=0), twist


def table_slices(side):
    rows = half_rows(side)
    sizes = ((2 * side, 2 * side),) * 2 + ((2 * rows, 3 * side // 2),) + ((side // 2, 2 * rows),) * 2
    starts = np.cumsum([0] + [size[0] for size in sizes])
    return [
        (slice(int(start), int(start) + height), slice(0, width))
        for start, (height, width) in zip(starts, sizes)
    ]


def halves(values):
    high = values.astype(jnp.bfloat16)
    low = (values - high.astype(jnp.float32)).astype(jnp.bfloat16)
    return high, low


def matmul(left, right):
    return jnp.dot(left, right, preferred_element_type=jnp.float32)


def gate_kernel(
    query, key_in, value, grad_out, filters, skip, tables, twist,
    sent, inputs, gains, tables_held, twist_held, taps, sems,
):
    slots, groups, length = query.shape
    per_row = length // LANES
    pieces = 3 * per_row
    pairs = [(source, inputs.at[place]) for place, source in enumerate((query, key_in, grad_out, value))]
    pairs += [(filters, taps), (skip, gains), (tables, tables_held), (twist, twist_held)]
    copies = [pltpu.make_async_copy(*pair, sems.at[place]) for place, pair in enumerate(pairs)]
    for copy in copies:
        copy.start()
    for copy in copies[:5]:
        copy.wait()
    back = lax.rem(groups - lax.axis_index("chan"), groups)
    taps_turned = pltpu.roll(taps[...], back, 0)
    for slot in range(slots):
        query_f, key_f, cotangent, value_f = [inputs[place, slot].astype(jnp.float32) for place in range(4)]
        base = pieces * groups * slot
        gated = pltpu.roll(query_f * key_f, back, 0)
        signal = pltpu.roll(cotangent * value_f, back, 0)
        for which, rows in enumerate((gated, signal, taps_turned)):
            for part in range(per_row):
                place = pl.ds(base + which * per_row + part, groups, stride=pieces)
                sent[place, :] = rows[:, part * LANES : (part + 1) * LANES]
    for copy in copies[5:]:
        copy.wait()


def spectral_kernel(side, parts, signals, combine, got, tables, twist, sent):
    mix_high, mix_low, first, last_high, last_low = [tables[place] for place in table_slices(side)]
    rows = half_rows(side)
    per_row = side // 2 // parts
    pieces = 3 * per_row

    def one(which):
        return jnp.concatenate(
            [got[pl.ds(which * per_row + part, parts, stride=pieces), :] for part in range(per_row)], axis=0
        )

    def turned(real, imag):
        return real * twist[0] - imag * twist[1], real * twist[1] + imag * twist[0]

    def mixed(pairs):
        high, low = halves(jnp.concatenate([jnp.concatenate(pair, axis=1) for pair in pairs], axis=0))
        values = matmul(high, mix_high) + (matmul(low, mix_high) + matmul(high, mix_low))
        blocks = [values[place * rows : (place + 1) * rows] for place in range(len(pairs))]
        return [(block[:, :side], block[:, side:]) for block in blocks]

    high, low = halves(jnp.concatenate([one(which) for which in signals], axis=1))
    coarse = matmul(first, jnp.concatenate([high, low, high], axis=0))
    lanes = [slice(place * side, (place + 1) * side) for place in range(len(signals))]
    spectra = mixed([turned(coarse[:rows, lane], coarse[rows:, lane]) for lane in lanes])
    products = [turned(*pair) for pair in mixed(combine(*spectra))]
    high, low = halves(
        jnp.concatenate([jnp.concatenate(parts_of, axis=1) for parts_of in zip(*products)], axis=0)
    )
    result = matmul(last_high, high) + (matmul(last_high, low) + matmul(last_low, high))
    spread = sent.shape[0] > side // 2
    for which in range(len(products)):
        for part in range(per_row):
            piece = result[part * parts : (part + 1) * parts, which * side : (which + 1) * side]
            if spread:
                sent[pl.ds(which * per_row + part, parts, stride=pieces), :] = piece
            else:
                sent[pl.ds(part * parts, parts), :] = piece


def lag_product(gated, signal):
    (gated_re, gated_im), (signal_re, signal_im) = gated, signal
    return [(gated_re * signal_re + gated_im * signal_im, gated_im * signal_re - gated_re * signal_im)]


def filtered(gated, signal, taps):
    (gated_re, gated_im), (signal_re, signal_im), (taps_re, taps_im) = gated, signal, taps
    conv = (taps_re * gated_re - taps_im * gated_im, -(taps_re * gated_im + taps_im * gated_re))
    corr = (taps_re * signal_re + taps_im * signal_im, taps_im * signal_re - taps_re * signal_im)
    return [conv, corr]


def pack_kernel(parts, rows, lags, sent):
    per_row = lags.shape[0] // parts
    pieces = sent.shape[0] // parts
    for part in range(per_row):
        sent[pl.ds(2 * per_row + part, parts, stride=pieces), :] = lags[pl.ds(part * parts, parts), :]


def grads_kernel(scale, got, inputs, skip, query_grad, key_grad, value_grad, filter_grad):
    _, slots, groups, length = inputs.shape
    per_row = length // LANES
    pieces = 3 * per_row
    ahead = lax.axis_index("chan")
    shape = (groups, groups)
    diagonal = lax.broadcasted_iota(jnp.int32, shape, 0) == lax.broadcasted_iota(jnp.int32, shape, 1)
    for slot in range(slots):
        gains = jnp.broadcast_to(skip[slot : slot + 1, :], shape)
        gain = jnp.sum(jnp.where(diagonal, gains, 0.0), axis=1, keepdims=True)
        base = slot * pieces * groups
        for part in range(per_row):
            lanes = slice(part * LANES, (part + 1) * LANES)
            conv = pltpu.roll(got[pl.ds(base + part, groups, stride=pieces), :], ahead, 0)
            corr = pltpu.roll(got[pl.ds(base + per_row + part, groups, stride=pieces), :], ahead, 0)
            query_f, key_f, cotangent, value_f = [
                inputs[place, slot, :, lanes].astype(jnp.float32) for place in range(4)
            ]
            out_field = conv + gain * (query_f * key_f)
            adjoint = corr + gain * (cotangent * value_f)
            query_grad[slot, :, lanes] = (adjoint * key_f).astype(jnp.bfloat16)
            key_grad[slot, :, lanes] = (adjoint * query_f).astype(jnp.bfloat16)
            value_grad[slot, :, lanes] = (cotangent * out_field).astype(jnp.bfloat16)
    for part in range(per_row):
        lagged = got[pl.ds(2 * per_row + part, slots * groups, stride=pieces), :]
        filter_grad[:, part * LANES : (part + 1) * LANES] = scale * jnp.sum(lagged, axis=0, keepdims=True)


def on_device(kernel, shapes, count, space=VMEM, scratch=(), aliases=None):
    outs = jax.tree.map(lambda shape: VMEM, shapes)
    return pl.pallas_call(
        kernel,
        out_shape=shapes,
        in_specs=[space] * count,
        out_specs=outs,
        scratch_shapes=scratch,
        input_output_aliases=aliases or {},
        compiler_params=pltpu.CompilerParams(vmem_limit_bytes=LIMIT),
    )


def in_hbm(array):
    return pltpu.with_memory_space_constraint(jnp.asarray(array), pltpu.HBM)


def exchange(rows, axis, count):
    blocks = rows.reshape(count, 1, rows.size // count)
    return lax.all_to_all(blocks, axis, 0, 0, tiled=True).reshape(rows.shape)


def local(query, key_in, value, grad_out, filters, skip):
    parts = lax.axis_size("seq")
    chans = lax.axis_size("chan")
    slots, groups, length = query.shape
    total = parts * length
    side = math.isqrt(2 * total)
    pieces = 3 * length // LANES
    packed = jax.ShapeDtypeStruct((parts * pieces, LANES), jnp.float32)
    tables, twist = fourier_tables(side, parts)
    shapes = (
        packed,
        jax.ShapeDtypeStruct((4, *query.shape), query.dtype),
        *[jax.ShapeDtypeStruct(array.shape, array.dtype) for array in (skip, tables, twist)],
    )
    scratch = [pltpu.VMEM(filters.shape, jnp.float32), pltpu.SemaphoreType.DMA((8,))]
    sent, inputs, gains, tables, twist = on_device(gate_kernel, shapes, 8, HBM, scratch)(
        *[in_hbm(array) for array in (query, key_in, value, grad_out, filters, skip, tables, twist)]
    )
    got = exchange(sent, "seq", parts)
    lag_rows = jax.ShapeDtypeStruct((side // 2, LANES), jnp.float32)
    lags = functools.partial(spectral_kernel, side, parts, (0, 1), lag_product)
    lags = on_device(lags, lag_rows, 3)(got, tables, twist)
    moves = [(s * chans + k, s * chans + (s + k) % chans) for s in range(parts) for k in range(chans)]
    lags = lax.ppermute(lags, ("seq", "chan"), moves)
    rows = functools.partial(spectral_kernel, side, parts, (0, 1, 2), filtered)
    rows = on_device(rows, packed, 3)(got, tables, twist)
    sent = on_device(functools.partial(pack_kernel, parts), packed, 2, aliases={0: 0})(rows, lags)
    got = exchange(sent, "seq", parts)
    grad = jax.ShapeDtypeStruct(query.shape, jnp.bfloat16)
    row = jax.ShapeDtypeStruct((1, length), jnp.float32)
    scale = 1.0 / math.sqrt(slots * chans * total)
    grads = functools.partial(grads_kernel, scale)
    return on_device(grads, (grad, grad, grad, row), 3)(got, inputs, gains)


def solution(mesh):
    spread = P("chan", None, "seq")
    return jax.shard_map(
        local,
        mesh=mesh,
        in_specs=(spread, spread, spread, spread, P(None, "seq"), P("chan", None)),
        out_specs=(spread, spread, spread, P("chan", "seq")),
        check_vma=False,
    )
```

```python
import functools
import math

import jax
import jax.numpy as jnp
import ml_dtypes
import numpy as np
from jax import lax
from jax.experimental import pallas as pl
from jax.experimental.pallas import tpu as pltpu
from jax.sharding import PartitionSpec as P

LANES = 128
VMEM = pl.BlockSpec(memory_space=pltpu.VMEM)
HBM = pl.BlockSpec(memory_space=pltpu.HBM)
LIMIT = 16 * 1024 * 1024
COPIES = 2


def split_table(table):
    high = table.astype(ml_dtypes.bfloat16)
    low = (table - high.astype(np.float64)).astype(ml_dtypes.bfloat16)
    return high, low


def half_rows(side):
    return -(-(side // 2 + 1) // 8) * 8


def fourier_tables(side, parts):
    used = side // 2 + 1
    rows = half_rows(side)
    per_block = side // 2 // parts
    order = np.arange(side // 2).reshape(parts, per_block).T.reshape(-1)
    coarse = np.arange(used)
    angle = 2.0 * math.pi / side * (coarse[:, None] * order[None, :] % side)
    first = np.zeros((2, rows, side // 2))
    first[0, :used] = np.cos(angle)
    first[1, :used] = -np.sin(angle)
    first = first.reshape(2 * rows, side // 2)
    weight = np.full((used,), 2.0)
    weight[0] = weight[-1] = 1.0
    last = np.zeros((side // 2, 2, rows))
    last[:, 0, :used] = (weight[:, None] * np.cos(angle)).T / side**2
    last[:, 1, :used] = (weight[:, None] * np.sin(angle)).T / side**2
    last = last.reshape(per_block, parts // COPIES, COPIES, 2 * rows)
    last = last.transpose(2, 0, 1, 3).reshape(side // 2, 2 * rows)
    turn = 2.0 * math.pi / side**2 * (coarse[:, None] * np.arange(side)[None, :])
    twist = np.zeros((2, rows, side), np.float32)
    twist[0, :used] = np.cos(turn)
    twist[1, :used] = -np.sin(turn)
    fine = 2.0 * math.pi / side * (np.arange(side)[:, None] * np.arange(side)[None, :] % side)
    fine_re, fine_im = np.cos(fine), -np.sin(fine)
    mix = np.block([[fine_re, fine_im], [-fine_im, fine_re]])
    first_high, first_low = split_table(first)
    first = np.concatenate([first_high, first_high, first_low], axis=1)
    blocks = [*split_table(mix), first, *split_table(last)]
    wide = max(block.shape[1] for block in blocks)
    stacked = [np.pad(block, ((0, 0), (0, wide - block.shape[1]))) for block in blocks]
    return np.concatenate(stacked, axis=0), twist


def table_slices(side):
    rows = half_rows(side)
    sizes = ((2 * side, 2 * side),) * 2 + ((2 * rows, 3 * side // 2),) + ((side // 2, 2 * rows),) * 2
    starts = np.cumsum([0] + [size[0] for size in sizes])
    return [
        (slice(int(start), int(start) + height), slice(0, width))
        for start, (height, width) in zip(starts, sizes)
    ]


def halves(values):
    high = values.astype(jnp.bfloat16)
    low = (values - high.astype(jnp.float32)).astype(jnp.bfloat16)
    return high, low


def matmul(left, right):
    return jnp.dot(left, right, preferred_element_type=jnp.float32)


def gate_kernel(
    query, key_in, value, grad_out, filters, skip, tables, twist,
    sent, inputs, gains, tables_held, twist_held, taps, sems,
):
    slots, groups, length = query.shape
    per_row = length // LANES
    pairs = [(source, inputs.at[place]) for place, source in enumerate((query, key_in, grad_out, value))]
    pairs += [(filters, taps), (skip, gains), (tables, tables_held), (twist, twist_held)]
    copies = [pltpu.make_async_copy(*pair, sems.at[place]) for place, pair in enumerate(pairs)]
    for copy in copies:
        copy.start()
    for copy in copies[:5]:
        copy.wait()
    back = lax.rem(groups - lax.axis_index("chan"), groups)
    products = []
    for first, second in ((0, 1), (2, 3)):
        for slot in range(slots):
            products.append(inputs[first, slot].astype(jnp.float32) * inputs[second, slot].astype(jnp.float32))
    pieces = (len(products) + 1) * per_row
    for which, rows in enumerate((*products, taps[...])):
        rows = pltpu.roll(rows, back, 0)
        for part in range(per_row):
            for twin in range(COPIES):
                place = pl.ds(twin * pieces + which * per_row + part, groups, stride=COPIES * pieces)
                sent[place, :] = rows[:, part * LANES : (part + 1) * LANES]
    for copy in copies[5:]:
        copy.wait()


def spectral_kernel(side, parts, signals, combine, got, tables, twist, sent):
    tables_at = table_slices(side)
    mix_high, mix_low, first = [tables[place] for place in tables_at[:3]]
    rows = half_rows(side)
    per_row = side // 2 // parts
    pieces = got.shape[0] // parts
    count = parts // COPIES
    mine = per_row * count
    twin = lax.rem(lax.axis_index("seq"), COPIES)
    last_high, last_low = [
        tables[pl.ds(pl.multiple_of(place.start + twin * mine, mine), mine), lanes] for place, lanes in tables_at[3:]
    ]

    def one(which):
        return jnp.concatenate(
            [got[pl.ds(which * per_row + part, parts, stride=pieces), :] for part in range(per_row)], axis=0
        )

    def turned(real, imag):
        return real * twist[0] - imag * twist[1], real * twist[1] + imag * twist[0]

    def mixed(pairs):
        high, low = halves(jnp.concatenate([jnp.concatenate(pair, axis=1) for pair in pairs], axis=0))
        values = matmul(high, mix_high) + (matmul(low, mix_high) + matmul(high, mix_low))
        blocks = [values[place * rows : (place + 1) * rows] for place in range(len(pairs))]
        return [(block[:, :side], block[:, side:]) for block in blocks]

    high, low = halves(jnp.concatenate([one(which) for which in range(signals)], axis=1))
    coarse = matmul(first, jnp.concatenate([high, low, high], axis=0))
    lanes = [slice(place * side, (place + 1) * side) for place in range(signals)]
    spectra = mixed([turned(coarse[:rows, lane], coarse[rows:, lane]) for lane in lanes])
    products = [turned(*pair) for pair in mixed(combine(*spectra))]
    high, low = halves(
        jnp.concatenate([jnp.concatenate(parts_of, axis=1) for parts_of in zip(*products)], axis=0)
    )
    result = matmul(last_high, high) + (matmul(last_high, low) + matmul(last_low, high))
    spread = sent.shape[0] > mine
    for which in range(len(products)):
        for part in range(per_row):
            piece = result[part * count : (part + 1) * count, which * side : (which + 1) * side]
            if spread:
                sent[pl.ds(which * per_row + part, count, stride=pieces), :] = piece
            else:
                sent[pl.ds(part * count, count), :] = piece


def lag_product(*spectra):
    real = imag = 0.0
    half = len(spectra) // 2
    for (gated_re, gated_im), (signal_re, signal_im) in zip(spectra[:half], spectra[half:]):
        real += gated_re * signal_re + gated_im * signal_im
        imag += gated_im * signal_re - gated_re * signal_im
    return [(real, imag)]


def filtered(*spectra):
    half = len(spectra) // 2
    taps_re, taps_im = spectra[-1]
    conv = [(taps_re * re - taps_im * im, -(taps_re * im + taps_im * re)) for re, im in spectra[:half]]
    corr = [(taps_re * re + taps_im * im, taps_im * re - taps_re * im) for re, im in spectra[half:-1]]
    return conv + corr


def pack_kernel(count, rows, lags, sent):
    per_row = lags.shape[0] // count
    pieces = sent.shape[0] // count
    for part in range(per_row):
        sent[pl.ds(pieces - per_row + part, count, stride=pieces), :] = lags[pl.ds(part * count, count), :]


def grads_kernel(scale, got, inputs, skip, query_grad, key_grad, value_grad, filter_grad):
    _, slots, groups, length = inputs.shape
    per_row = length // LANES
    pieces = (2 * slots + 1) * per_row
    ahead = lax.axis_index("chan")
    shape = (groups, groups)
    diagonal = lax.broadcasted_iota(jnp.int32, shape, 0) == lax.broadcasted_iota(jnp.int32, shape, 1)
    for slot in range(slots):
        gains = jnp.broadcast_to(skip[slot : slot + 1, :], shape)
        gain = jnp.sum(jnp.where(diagonal, gains, 0.0), axis=1, keepdims=True)
        for part in range(per_row):
            lanes = slice(part * LANES, (part + 1) * LANES)
            base = slot * per_row + part
            conv = pltpu.roll(got[pl.ds(base, groups, stride=pieces), :], ahead, 0)
            corr = pltpu.roll(got[pl.ds(base + slots * per_row, groups, stride=pieces), :], ahead, 0)
            query_f, key_f, cotangent, value_f = [
                inputs[place, slot, :, lanes].astype(jnp.float32) for place in range(4)
            ]
            out_field = conv + gain * (query_f * key_f)
            adjoint = corr + gain * (cotangent * value_f)
            query_grad[slot, :, lanes] = (adjoint * key_f).astype(jnp.bfloat16)
            key_grad[slot, :, lanes] = (adjoint * query_f).astype(jnp.bfloat16)
            value_grad[slot, :, lanes] = (cotangent * out_field).astype(jnp.bfloat16)
    for part in range(per_row):
        lagged = got[pl.ds(2 * slots * per_row + part, groups, stride=pieces), :]
        filter_grad[:, part * LANES : (part + 1) * LANES] = scale * jnp.sum(lagged, axis=0, keepdims=True)


def on_device(kernel, shapes, count, space=VMEM, scratch=(), aliases=None):
    outs = jax.tree.map(lambda shape: VMEM, shapes)
    return pl.pallas_call(
        kernel,
        out_shape=shapes,
        in_specs=[space] * count,
        out_specs=outs,
        scratch_shapes=scratch,
        input_output_aliases=aliases or {},
        compiler_params=pltpu.CompilerParams(vmem_limit_bytes=LIMIT),
    )


def in_hbm(array):
    return pltpu.with_memory_space_constraint(jnp.asarray(array), pltpu.HBM)


def exchange(rows, axis, count, among=None):
    blocks = rows.reshape(count, 1, rows.size // count)
    return lax.all_to_all(blocks, axis, 0, 0, tiled=True, axis_index_groups=among).reshape(rows.shape)


def local(query, key_in, value, grad_out, filters, skip):
    parts = lax.axis_size("seq")
    chans = lax.axis_size("chan")
    slots, groups, length = query.shape
    total = parts * length
    side = math.isqrt(2 * total)
    pieces = (2 * slots + 1) * length // LANES
    count = parts // COPIES
    packed = jax.ShapeDtypeStruct((parts * pieces, LANES), jnp.float32)
    tables, twist = fourier_tables(side, parts)
    shapes = (
        packed,
        jax.ShapeDtypeStruct((4, *query.shape), query.dtype),
        *[jax.ShapeDtypeStruct(array.shape, array.dtype) for array in (skip, tables, twist)],
    )
    scratch = [pltpu.VMEM(filters.shape, jnp.float32), pltpu.SemaphoreType.DMA((8,))]
    sent, inputs, gains, tables, twist = on_device(gate_kernel, shapes, 8, HBM, scratch)(
        *[in_hbm(array) for array in (query, key_in, value, grad_out, filters, skip, tables, twist)]
    )
    got = exchange(sent, "seq", parts)
    lag_rows = jax.ShapeDtypeStruct((side // 2 // COPIES, LANES), jnp.float32)
    lags = functools.partial(spectral_kernel, side, parts, 2 * slots, lag_product)
    lags = on_device(lags, lag_rows, 3)(got, tables, twist)
    moves = [
        (s * chans + k, s * chans + (s // COPIES + k) % chans) for s in range(parts) for k in range(chans)
    ]
    lags = lax.ppermute(lags, ("seq", "chan"), moves)
    packed = jax.ShapeDtypeStruct((count * pieces, LANES), jnp.float32)
    rows = functools.partial(spectral_kernel, side, parts, 2 * slots + 1, filtered)
    rows = on_device(rows, packed, 3)(got, tables, twist)
    sent = on_device(functools.partial(pack_kernel, count), packed, 2, aliases={0: 0})(rows, lags)
    got = exchange(sent, "seq", count, [list(range(twin, parts, COPIES)) for twin in range(COPIES)])
    grad = jax.ShapeDtypeStruct(query.shape, jnp.bfloat16)
    row = jax.ShapeDtypeStruct((1, length), jnp.float32)
    scale = 1.0 / math.sqrt(slots * chans * total)
    grads = functools.partial(grads_kernel, scale)
    return on_device(grads, (grad, grad, grad, row), 3)(got, inputs, gains)


def solution(mesh):
    spread = P("chan", None, "seq")
    return jax.shard_map(
        local,
        mesh=mesh,
        in_specs=(spread, spread, spread, spread, P(None, "seq"), P("chan", None)),
        out_specs=(spread, spread, spread, P("chan", "seq")),
        check_vma=False,
    )
```

```python
import functools
import math

import jax
import jax.numpy as jnp
import ml_dtypes
import numpy as np
from jax import lax
from jax.experimental import pallas as pl
from jax.experimental.pallas import tpu as pltpu
from jax.sharding import PartitionSpec as P

LANES = 128
VMEM = pl.BlockSpec(memory_space=pltpu.VMEM)
HBM = pl.BlockSpec(memory_space=pltpu.HBM)
LIMIT = 16 * 1024 * 1024
COPIES = 2


def split_table(table):
    high = table.astype(ml_dtypes.bfloat16)
    low = (table - high.astype(np.float64)).astype(ml_dtypes.bfloat16)
    return high, low


def half_rows(side):
    return -(-(side // 2 + 1) // 8) * 8


def fourier_tables(side, parts):
    used = side // 2 + 1
    rows = half_rows(side)
    per_block = side // 2 // parts
    order = np.arange(side // 2).reshape(parts, per_block).T.reshape(-1)
    coarse = np.arange(used)
    angle = 2.0 * math.pi / side * (coarse[:, None] * order[None, :] % side)
    first = np.zeros((2, rows, side // 2))
    first[0, :used] = np.cos(angle)
    first[1, :used] = -np.sin(angle)
    first = first.reshape(2 * rows, side // 2)
    weight = np.full((used,), 2.0)
    weight[0] = weight[-1] = 1.0
    last = np.zeros((side // 2, 2, rows))
    last[:, 0, :used] = (weight[:, None] * np.cos(angle)).T / side**2
    last[:, 1, :used] = (weight[:, None] * np.sin(angle)).T / side**2
    last = last.reshape(per_block, parts // COPIES, COPIES, 2 * rows)
    last = last.transpose(2, 0, 1, 3).reshape(side // 2, 2 * rows)
    turn = 2.0 * math.pi / side**2 * (coarse[:, None] * np.arange(side)[None, :])
    twist = np.zeros((2, rows, side))
    twist[0, :used] = np.cos(turn)
    twist[1, :used] = -np.sin(turn)
    fine = 2.0 * math.pi / side * (np.arange(side)[:, None] * np.arange(side)[None, :] % side)
    fine_re, fine_im = np.cos(fine), -np.sin(fine)
    fine = np.concatenate([fine_re, fine_im], axis=1)
    twist = np.concatenate([twist[0], twist[1]], axis=1)
    first_high, first_low = split_table(first)
    first = np.concatenate([first_high, first_high, first_low], axis=1)
    blocks = [*split_table(fine), first, *split_table(last), *split_table(twist)]
    wide = max(block.shape[1] for block in blocks)
    stacked = [np.pad(block, ((0, -block.shape[0] % 16), (0, wide - block.shape[1]))) for block in blocks]
    return np.concatenate(stacked, axis=0)


def table_slices(side):
    rows = half_rows(side)
    sizes = ((side, 2 * side),) * 2 + ((2 * rows, 3 * side // 2),) + ((side // 2, 2 * rows),) * 2 + ((rows, 2 * side),) * 2
    starts = np.cumsum([0] + [-(-size[0] // 16) * 16 for size in sizes])
    return [
        (slice(int(start), int(start) + height), slice(0, width))
        for start, (height, width) in zip(starts, sizes)
    ]


def halves(values):
    high = values.astype(jnp.bfloat16)
    low = (values - high.astype(jnp.float32)).astype(jnp.bfloat16)
    return high, low


def matmul(left, right):
    return jnp.dot(left, right, preferred_element_type=jnp.float32)


def gate_kernel(
    query, key_in, value, grad_out, filters, tables,
    sent, inputs, tables_held, taps, sems,
):
    slots, groups, length = query.shape
    per_row = length // LANES
    pairs = [(source, inputs.at[place]) for place, source in enumerate((query, key_in, grad_out, value))]
    pairs += [(filters, taps), (tables, tables_held)]
    copies = [pltpu.make_async_copy(*pair, sems.at[place]) for place, pair in enumerate(pairs)]
    for copy in (copies[5], *copies[:5]):
        copy.start()
    back = lax.rem(groups - lax.axis_index("chan"), groups)
    products = []
    for first, second in ((0, 1), (2, 3)):
        copies[first].wait()
        copies[second].wait()
        for slot in range(slots):
            products.append(inputs[first, slot].astype(jnp.float32) * inputs[second, slot].astype(jnp.float32))
    pieces = (len(products) + 1) * per_row
    copies[4].wait()
    for which, rows in enumerate((*products, taps[...])):
        rows = pltpu.roll(rows, back, 0)
        for part in range(per_row):
            for twin in range(COPIES):
                place = pl.ds(twin * pieces + which * per_row + part, groups, stride=COPIES * pieces)
                sent[place, :] = rows[:, part * LANES : (part + 1) * LANES]
    for copy in copies[5:]:
        copy.wait()


def spectral_kernel(side, parts, signals, combine, got, tables, sent):
    tables_at = table_slices(side)
    fine_high, fine_low, first = [tables[place] for place in tables_at[:3]]
    twist_high, twist_low = [tables[place].astype(jnp.float32) for place in tables_at[5:]]
    twist = twist_high + twist_low
    turn_re, turn_im = twist[:, :side], twist[:, side:]
    mix_high, mix_low = [
        jnp.concatenate([table, jnp.concatenate([-table[:, side:], table[:, :side]], axis=1)], axis=0)
        for table in (fine_high, fine_low)
    ]
    rows = half_rows(side)
    per_row = side // 2 // parts
    pieces = got.shape[0] // parts
    count = parts // COPIES
    mine = per_row * count
    twin = lax.rem(lax.axis_index("seq"), COPIES)
    last_high, last_low = [
        tables[pl.ds(pl.multiple_of(place.start + twin * mine, mine), mine), lanes] for place, lanes in tables_at[3:5]
    ]

    def one(which):
        return jnp.concatenate(
            [got[pl.ds(which * per_row + part, parts, stride=pieces), :] for part in range(per_row)], axis=0
        )

    def turned(real, imag):
        return real * turn_re - imag * turn_im, real * turn_im + imag * turn_re

    def mixed(pairs):
        stack = jnp.concatenate([jnp.concatenate(pair, axis=1) for pair in pairs], axis=0)
        high = stack.astype(jnp.bfloat16).astype(jnp.float32)
        both = matmul(jnp.concatenate([high, stack - high], axis=0).astype(jnp.bfloat16), mix_high)
        height = stack.shape[0]
        values = both[:height] + (both[height:] + matmul(high.astype(jnp.bfloat16), mix_low))
        blocks = [values[place * rows : (place + 1) * rows] for place in range(len(pairs))]
        return [(block[:, :side], block[:, side:]) for block in blocks]

    high, low = halves(jnp.concatenate([one(which) for which in range(signals)], axis=1))
    coarse = matmul(first, jnp.concatenate([high, low, high], axis=0))
    lanes = [slice(place * side, (place + 1) * side) for place in range(signals)]
    spectra = mixed([turned(coarse[:rows, lane], coarse[rows:, lane]) for lane in lanes])
    products = [turned(*pair) for pair in mixed(combine(*spectra))]
    high, low = halves(
        jnp.concatenate([jnp.concatenate(parts_of, axis=1) for parts_of in zip(*products)], axis=0)
    )
    result = matmul(last_high, high) + (matmul(last_high, low) + matmul(last_low, high))
    spread = sent.shape[0] > mine
    for which in range(len(products)):
        for part in range(per_row):
            piece = result[part * count : (part + 1) * count, which * side : (which + 1) * side]
            if spread:
                sent[pl.ds(which * per_row + part, count, stride=pieces), :] = piece
            else:
                sent[pl.ds(part * count, count), :] = piece


def lag_product(*spectra):
    real = imag = 0.0
    half = len(spectra) // 2
    for (gated_re, gated_im), (signal_re, signal_im) in zip(spectra[:half], spectra[half:]):
        real += gated_re * signal_re + gated_im * signal_im
        imag += gated_im * signal_re - gated_re * signal_im
    return [(real, imag)]


def filtered(*spectra):
    half = len(spectra) // 2
    taps_re, taps_im = spectra[-1]
    conv = [(taps_re * re - taps_im * im, -(taps_re * im + taps_im * re)) for re, im in spectra[:half]]
    corr = [(taps_re * re + taps_im * im, taps_im * re - taps_re * im) for re, im in spectra[half:-1]]
    return conv + corr


def pack_kernel(count, rows, lags, sent):
    per_row = lags.shape[0] // count
    pieces = sent.shape[0] // count
    for part in range(per_row):
        sent[pl.ds(pieces - per_row + part, count, stride=pieces), :] = lags[pl.ds(part * count, count), :]


def filter_kernel(spectral, got, tables, skip, sent, gains, sem):
    copy = pltpu.make_async_copy(skip, gains, sem)
    copy.start()
    spectral(got, tables, sent)
    copy.wait()


def grads_kernel(scale, got, inputs, skip, query_grad, key_grad, value_grad, filter_grad):
    _, slots, groups, length = inputs.shape
    per_row = length // LANES
    pieces = (2 * slots + 1) * per_row
    ahead = lax.axis_index("chan")
    shape = (groups, groups)
    diagonal = lax.broadcasted_iota(jnp.int32, shape, 0) == lax.broadcasted_iota(jnp.int32, shape, 1)
    for slot in range(slots):
        gains = jnp.broadcast_to(skip[slot : slot + 1, :], shape)
        gain = jnp.sum(jnp.where(diagonal, gains, 0.0), axis=1, keepdims=True)
        for part in range(per_row):
            lanes = slice(part * LANES, (part + 1) * LANES)
            base = slot * per_row + part
            conv = pltpu.roll(got[pl.ds(base, groups, stride=pieces), :], ahead, 0)
            corr = pltpu.roll(got[pl.ds(base + slots * per_row, groups, stride=pieces), :], ahead, 0)
            query_f, key_f, cotangent, value_f = [
                inputs[place, slot, :, lanes].astype(jnp.float32) for place in range(4)
            ]
            out_field = conv + gain * (query_f * key_f)
            adjoint = corr + gain * (cotangent * value_f)
            query_grad[slot, :, lanes] = (adjoint * key_f).astype(jnp.bfloat16)
            key_grad[slot, :, lanes] = (adjoint * query_f).astype(jnp.bfloat16)
            value_grad[slot, :, lanes] = (cotangent * out_field).astype(jnp.bfloat16)
    for part in range(per_row):
        lagged = got[pl.ds(2 * slots * per_row + part, groups, stride=pieces), :]
        filter_grad[:, part * LANES : (part + 1) * LANES] = scale * jnp.sum(lagged, axis=0, keepdims=True)


def on_device(kernel, shapes, spaces, scratch=(), aliases=None, out_space=VMEM):
    outs = jax.tree.map(lambda shape: out_space, shapes)
    return pl.pallas_call(
        kernel,
        out_shape=shapes,
        in_specs=spaces,
        out_specs=outs,
        scratch_shapes=scratch,
        input_output_aliases=aliases or {},
        compiler_params=pltpu.CompilerParams(vmem_limit_bytes=LIMIT),
    )


def in_hbm(array):
    return pltpu.with_memory_space_constraint(jnp.asarray(array), pltpu.HBM)


def exchange(rows, axis, count, among=None):
    blocks = rows.reshape(count, 1, rows.size // count)
    return lax.all_to_all(blocks, axis, 0, 0, tiled=True, axis_index_groups=among).reshape(rows.shape)


def local(query, key_in, value, grad_out, filters, skip):
    parts = lax.axis_size("seq")
    chans = lax.axis_size("chan")
    slots, groups, length = query.shape
    total = parts * length
    side = math.isqrt(2 * total)
    pieces = (2 * slots + 1) * length // LANES
    count = parts // COPIES
    packed = jax.ShapeDtypeStruct((parts * pieces, LANES), jnp.float32)
    tables = fourier_tables(side, parts)
    shapes = (
        packed,
        jax.ShapeDtypeStruct((4, *query.shape), query.dtype),
        jax.ShapeDtypeStruct(tables.shape, tables.dtype),
    )
    scratch = [pltpu.VMEM(filters.shape, jnp.float32), pltpu.SemaphoreType.DMA((6,))]
    sent, inputs, tables = on_device(gate_kernel, shapes, [HBM] * 6, scratch)(
        *[in_hbm(array) for array in (query, key_in, value, grad_out, filters, tables)]
    )
    got = exchange(sent, "seq", parts)
    lag_rows = jax.ShapeDtypeStruct((side // 2 // COPIES, LANES), jnp.float32)
    lags = functools.partial(spectral_kernel, side, parts, 2 * slots, lag_product)
    lags = on_device(lags, lag_rows, [VMEM] * 2)(got, tables)
    moves = [
        (s * chans + k, s * chans + (s // COPIES + k) % chans) for s in range(parts) for k in range(chans)
    ]
    lags = lax.ppermute(lags, ("seq", "chan"), moves)
    packed = jax.ShapeDtypeStruct((count * pieces, LANES), jnp.float32)
    rows = functools.partial(spectral_kernel, side, parts, 2 * slots + 1, filtered)
    held = jax.ShapeDtypeStruct(skip.shape, skip.dtype)
    rows = functools.partial(filter_kernel, rows)
    rows, gains = on_device(rows, (packed, held), [VMEM, VMEM, HBM], [pltpu.SemaphoreType.DMA])(
        got, tables, in_hbm(skip)
    )
    sent = on_device(functools.partial(pack_kernel, count), packed, [VMEM] * 2, aliases={0: 0})(rows, lags)
    got = exchange(sent, "seq", count, [list(range(twin, parts, COPIES)) for twin in range(COPIES)])
    grad = jax.ShapeDtypeStruct(query.shape, jnp.bfloat16)
    row = jax.ShapeDtypeStruct((1, length), jnp.float32)
    scale = 1.0 / math.sqrt(slots * chans * total)
    grads = functools.partial(grads_kernel, scale)
    return on_device(grads, (grad, grad, grad, row), [VMEM] * 3)(got, inputs, gains)


def solution(mesh):
    spread = P("chan", None, "seq")
    return jax.shard_map(
        local,
        mesh=mesh,
        in_specs=(spread, spread, spread, spread, P(None, "seq"), P("chan", None)),
        out_specs=(spread, spread, spread, P("chan", "seq")),
        check_vma=False,
    )
```

```python
import functools
import math

import jax
import jax.numpy as jnp
import ml_dtypes
import numpy as np
from jax import lax
from jax.experimental import pallas as pl
from jax.experimental.pallas import tpu as pltpu
from jax.sharding import PartitionSpec as P

LANES = 128
VMEM = pl.BlockSpec(memory_space=pltpu.VMEM)
HBM = pl.BlockSpec(memory_space=pltpu.HBM)
LIMIT = 16 * 1024 * 1024
COPIES = 2


def split_table(table):
    high = table.astype(ml_dtypes.bfloat16)
    low = (table - high.astype(np.float64)).astype(ml_dtypes.bfloat16)
    return high, low


def half_rows(side):
    return -(-(side // 2 + 1) // 8) * 8


def fourier_tables(side, parts):
    used = side // 2 + 1
    rows = half_rows(side)
    per_block = side // 2 // parts
    order = np.arange(side // 2).reshape(parts, per_block).T.reshape(-1)
    coarse = np.arange(used)
    angle = 2.0 * math.pi / side * (coarse[:, None] * order[None, :] % side)
    first = np.zeros((2, rows, side // 2))
    first[0, :used] = np.cos(angle)
    first[1, :used] = -np.sin(angle)
    first = first.reshape(2 * rows, side // 2)
    weight = np.full((used,), 2.0)
    weight[0] = weight[-1] = 1.0
    last = np.zeros((side // 2, 2, rows))
    last[:, 0, :used] = (weight[:, None] * np.cos(angle)).T / side**2
    last[:, 1, :used] = (weight[:, None] * np.sin(angle)).T / side**2
    last = last.reshape(per_block, parts // COPIES, COPIES, 2 * rows)
    last = last.transpose(2, 0, 1, 3).reshape(side // 2, 2 * rows)
    turn = 2.0 * math.pi / side**2 * (coarse[:, None] * np.arange(side)[None, :])
    twist = np.zeros((2, rows, side))
    twist[0, :used] = np.cos(turn)
    twist[1, :used] = -np.sin(turn)
    fine = 2.0 * math.pi / side * (np.arange(side)[:, None] * np.arange(side)[None, :] % side)
    fine_re, fine_im = np.cos(fine), -np.sin(fine)
    fine = np.concatenate([fine_re, fine_im], axis=1)
    twist = np.concatenate([twist[0], twist[1]], axis=1)
    first_high, first_low = split_table(first)
    first = np.concatenate([first_high, first_high, first_low], axis=1)
    blocks = [*split_table(fine), first, *split_table(last), *split_table(twist)]
    wide = max(block.shape[1] for block in blocks)
    stacked = [np.pad(block, ((0, -block.shape[0] % 16), (0, wide - block.shape[1]))) for block in blocks]
    return np.concatenate(stacked, axis=0)


def table_slices(side):
    rows = half_rows(side)
    sizes = ((side, 2 * side),) * 2 + ((2 * rows, 3 * side // 2),) + ((side // 2, 2 * rows),) * 2 + ((rows, 2 * side),) * 2
    starts = np.cumsum([0] + [-(-size[0] // 16) * 16 for size in sizes])
    return [
        (slice(int(start), int(start) + height), slice(0, width))
        for start, (height, width) in zip(starts, sizes)
    ]


def halves(values):
    high = values.astype(jnp.bfloat16)
    low = (values - high.astype(jnp.float32)).astype(jnp.bfloat16)
    return high, low


def matmul(left, right):
    return jnp.dot(left, right, preferred_element_type=jnp.float32)


def gate_kernel(
    query, key_in, value, grad_out, filters, tables,
    sent, inputs, tables_held, taps, sems,
):
    slots, groups, length = query.shape
    per_row = length // LANES
    pairs = [(source, inputs.at[place]) for place, source in enumerate((query, key_in, grad_out, value))]
    pairs += [(filters, taps), (tables, tables_held)]
    copies = [pltpu.make_async_copy(*pair, sems.at[place]) for place, pair in enumerate(pairs)]
    for copy in (copies[5], *copies[:5]):
        copy.start()
    ahead = lax.axis_index("chan")
    products = []
    for first, second in ((0, 1), (2, 3)):
        copies[first].wait()
        copies[second].wait()
        for slot in range(slots):
            products.append(inputs[first, slot].astype(jnp.float32) * inputs[second, slot].astype(jnp.float32))
    pieces = (len(products) + 1) * per_row
    copies[4].wait()
    for which, rows in enumerate((*products, taps[...])):
        rows = pltpu.roll(rows, ahead, 0)
        for part in range(per_row):
            for twin in range(COPIES):
                place = pl.ds(twin * pieces + which * per_row + part, groups, stride=COPIES * pieces)
                sent[place, :] = rows[:, part * LANES : (part + 1) * LANES]
    for copy in copies[5:]:
        copy.wait()


def spectral_kernel(side, parts, signals, combine, got, tables, sent):
    tables_at = table_slices(side)
    fine_high, fine_low, first = [tables[place] for place in tables_at[:3]]
    twist_high, twist_low = [tables[place].astype(jnp.float32) for place in tables_at[5:]]
    twist = twist_high + twist_low
    turn_re, turn_im = twist[:, :side], twist[:, side:]
    mix_high, mix_low = [
        jnp.concatenate([table, jnp.concatenate([-table[:, side:], table[:, :side]], axis=1)], axis=0)
        for table in (fine_high, fine_low)
    ]
    rows = half_rows(side)
    per_row = side // 2 // parts
    pieces = got.shape[0] // parts
    count = parts // COPIES
    mine = per_row * count
    twin = lax.rem(lax.axis_index("seq"), COPIES)
    last_high, last_low = [
        tables[pl.ds(pl.multiple_of(place.start + twin * mine, mine), mine), lanes] for place, lanes in tables_at[3:5]
    ]

    def one(which):
        return jnp.concatenate(
            [got[pl.ds(which * per_row + part, parts, stride=pieces), :] for part in range(per_row)], axis=0
        )

    def turned(real, imag):
        return real * turn_re - imag * turn_im, real * turn_im + imag * turn_re

    def mixed(pairs):
        stack = jnp.concatenate([jnp.concatenate(pair, axis=1) for pair in pairs], axis=0)
        high = stack.astype(jnp.bfloat16).astype(jnp.float32)
        both = matmul(jnp.concatenate([high, stack - high], axis=0).astype(jnp.bfloat16), mix_high)
        height = stack.shape[0]
        values = both[:height] + (both[height:] + matmul(high.astype(jnp.bfloat16), mix_low))
        blocks = [values[place * rows : (place + 1) * rows] for place in range(len(pairs))]
        return [(block[:, :side], block[:, side:]) for block in blocks]

    high, low = halves(jnp.concatenate([one(which) for which in range(signals)], axis=1))
    coarse = matmul(first, jnp.concatenate([high, low, high], axis=0))
    lanes = [slice(place * side, (place + 1) * side) for place in range(signals)]
    spectra = mixed([turned(coarse[:rows, lane], coarse[rows:, lane]) for lane in lanes])
    products = [turned(*pair) for pair in mixed(combine(*spectra))]
    high, low = halves(
        jnp.concatenate([jnp.concatenate(parts_of, axis=1) for parts_of in zip(*products)], axis=0)
    )
    result = matmul(last_high, high) + (matmul(last_high, low) + matmul(last_low, high))
    spread = sent.shape[0] > mine
    for which in range(len(products)):
        for part in range(per_row):
            piece = result[part * count : (part + 1) * count, which * side : (which + 1) * side]
            if spread:
                sent[pl.ds(which * per_row + part, count, stride=pieces), :] = piece
            else:
                sent[pl.ds(part * count, count), :] = piece


def lag_product(*spectra):
    real = imag = 0.0
    half = len(spectra) // 2
    for (gated_re, gated_im), (signal_re, signal_im) in zip(spectra[:half], spectra[half:]):
        real += gated_re * signal_re + gated_im * signal_im
        imag += gated_im * signal_re - gated_re * signal_im
    return [(real, imag)]


def filtered(*spectra):
    half = len(spectra) // 2
    taps_re, taps_im = spectra[-1]
    conv = [(taps_re * re - taps_im * im, -(taps_re * im + taps_im * re)) for re, im in spectra[:half]]
    corr = [(taps_re * re + taps_im * im, taps_im * re - taps_re * im) for re, im in spectra[half:-1]]
    return conv + corr


def pack_kernel(count, rows, lags, sent):
    per_row = lags.shape[0] // count
    pieces = sent.shape[0] // count
    for part in range(per_row):
        sent[pl.ds(pieces - per_row + part, count, stride=pieces), :] = lags[pl.ds(part * count, count), :]


def filter_kernel(spectral, got, tables, skip, sent, gains, sem):
    copy = pltpu.make_async_copy(skip, gains, sem)
    copy.start()
    spectral(got, tables, sent)
    copy.wait()


def grads_kernel(scale, got, inputs, skip, query_grad, key_grad, value_grad, filter_grad):
    _, slots, groups, length = inputs.shape
    per_row = length // LANES
    pieces = (2 * slots + 1) * per_row
    back = lax.rem(groups - lax.axis_index("chan"), groups)
    shape = (groups, groups)
    diagonal = lax.broadcasted_iota(jnp.int32, shape, 0) == lax.broadcasted_iota(jnp.int32, shape, 1)
    for slot in range(slots):
        gains = jnp.broadcast_to(skip[slot : slot + 1, :], shape)
        gain = jnp.sum(jnp.where(diagonal, gains, 0.0), axis=1, keepdims=True)
        for part in range(per_row):
            lanes = slice(part * LANES, (part + 1) * LANES)
            base = slot * per_row + part
            conv = pltpu.roll(got[pl.ds(base, groups, stride=pieces), :], back, 0)
            corr = pltpu.roll(got[pl.ds(base + slots * per_row, groups, stride=pieces), :], back, 0)
            query_f, key_f, cotangent, value_f = [
                inputs[place, slot, :, lanes].astype(jnp.float32) for place in range(4)
            ]
            out_field = conv + gain * (query_f * key_f)
            adjoint = corr + gain * (cotangent * value_f)
            query_grad[slot, :, lanes] = (adjoint * key_f).astype(jnp.bfloat16)
            key_grad[slot, :, lanes] = (adjoint * query_f).astype(jnp.bfloat16)
            value_grad[slot, :, lanes] = (cotangent * out_field).astype(jnp.bfloat16)
    for part in range(per_row):
        lagged = got[pl.ds(2 * slots * per_row + part, groups, stride=pieces), :]
        filter_grad[:, part * LANES : (part + 1) * LANES] = scale * jnp.sum(lagged, axis=0, keepdims=True)


def on_device(kernel, shapes, spaces, scratch=(), aliases=None, out_space=VMEM):
    outs = jax.tree.map(lambda shape: out_space, shapes)
    return pl.pallas_call(
        kernel,
        out_shape=shapes,
        in_specs=spaces,
        out_specs=outs,
        scratch_shapes=scratch,
        input_output_aliases=aliases or {},
        compiler_params=pltpu.CompilerParams(vmem_limit_bytes=LIMIT),
    )


def in_hbm(array):
    return pltpu.with_memory_space_constraint(jnp.asarray(array), pltpu.HBM)


def exchange(rows, axis, count, among=None):
    blocks = rows.reshape(count, 1, rows.size // count)
    return lax.all_to_all(blocks, axis, 0, 0, tiled=True, axis_index_groups=among).reshape(rows.shape)


def local(query, key_in, value, grad_out, filters, skip):
    parts = lax.axis_size("seq")
    chans = lax.axis_size("chan")
    slots, groups, length = query.shape
    total = parts * length
    side = math.isqrt(2 * total)
    pieces = (2 * slots + 1) * length // LANES
    count = parts // COPIES
    packed = jax.ShapeDtypeStruct((parts * pieces, LANES), jnp.float32)
    tables = fourier_tables(side, parts)
    shapes = (
        packed,
        jax.ShapeDtypeStruct((4, *query.shape), query.dtype),
        jax.ShapeDtypeStruct(tables.shape, tables.dtype),
    )
    scratch = [pltpu.VMEM(filters.shape, jnp.float32), pltpu.SemaphoreType.DMA((6,))]
    sent, inputs, tables = on_device(gate_kernel, shapes, [HBM] * 6, scratch)(
        *[in_hbm(array) for array in (query, key_in, value, grad_out, filters, tables)]
    )
    got = exchange(sent, "seq", parts)
    lag_rows = jax.ShapeDtypeStruct((side // 2 // COPIES, LANES), jnp.float32)
    lags = functools.partial(spectral_kernel, side, parts, 2 * slots, lag_product)
    lags = on_device(lags, lag_rows, [VMEM] * 2)(got, tables)
    moves = [
        (s * chans + k, s * chans + (s // COPIES - k) % chans) for s in range(parts) for k in range(chans)
    ]
    lags = lax.ppermute(lags, ("seq", "chan"), moves)
    packed = jax.ShapeDtypeStruct((count * pieces, LANES), jnp.float32)
    rows = functools.partial(spectral_kernel, side, parts, 2 * slots + 1, filtered)
    held = jax.ShapeDtypeStruct(skip.shape, skip.dtype)
    rows = functools.partial(filter_kernel, rows)
    rows, gains = on_device(rows, (packed, held), [VMEM, VMEM, HBM], [pltpu.SemaphoreType.DMA])(
        got, tables, in_hbm(skip)
    )
    sent = on_device(functools.partial(pack_kernel, count), packed, [VMEM] * 2, aliases={0: 0})(rows, lags)
    got = exchange(sent, "seq", count, [list(range(twin, parts, COPIES)) for twin in range(COPIES)])
    grad = jax.ShapeDtypeStruct(query.shape, jnp.bfloat16)
    row = jax.ShapeDtypeStruct((1, length), jnp.float32)
    scale = 1.0 / math.sqrt(slots * chans * total)
    grads = functools.partial(grads_kernel, scale)
    return on_device(grads, (grad, grad, grad, row), [VMEM] * 3)(got, inputs, gains)


def solution(mesh):
    spread = P("chan", None, "seq")
    return jax.shard_map(
        local,
        mesh=mesh,
        in_specs=(spread, spread, spread, spread, P(None, "seq"), P("chan", None)),
        out_specs=(spread, spread, spread, P("chan", "seq")),
        check_vma=False,
    )
```

```python
import functools
import math

import jax
import jax.numpy as jnp
import ml_dtypes
import numpy as np
from jax import lax
from jax.experimental import pallas as pl
from jax.experimental.pallas import tpu as pltpu
from jax.sharding import PartitionSpec as P

LANES = 128
VMEM = pl.BlockSpec(memory_space=pltpu.VMEM)
HBM = pl.BlockSpec(memory_space=pltpu.HBM)
LIMIT = 16 * 1024 * 1024
COPIES = 2


def split_table(table):
    high = table.astype(ml_dtypes.bfloat16)
    low = (table - high.astype(np.float64)).astype(ml_dtypes.bfloat16)
    return high, low


def half_rows(side):
    return -(-(side // 2 + 1) // 8) * 8


def fourier_tables(side, parts):
    used = side // 2 + 1
    rows = half_rows(side)
    per_block = side // 2 // parts
    order = np.arange(side // 2).reshape(parts, per_block).T.reshape(-1)
    coarse = np.arange(used)
    angle = 2.0 * math.pi / side * (coarse[:, None] * order[None, :] % side)
    first = np.zeros((2, rows, side // 2))
    first[0, :used] = np.cos(angle)
    first[1, :used] = -np.sin(angle)
    first = first.reshape(2 * rows, side // 2)
    weight = np.full((used,), 2.0)
    weight[0] = weight[-1] = 1.0
    last = np.zeros((side // 2, 2, rows))
    last[:, 0, :used] = (weight[:, None] * np.cos(angle)).T / side**2
    last[:, 1, :used] = (weight[:, None] * np.sin(angle)).T / side**2
    last = last.reshape(per_block, parts // COPIES, COPIES, 2 * rows)
    last = last.transpose(2, 0, 1, 3).reshape(side // 2, 2 * rows)
    turn = 2.0 * math.pi / side**2 * (coarse[:, None] * np.arange(side)[None, :])
    twist = np.zeros((2, rows, side))
    twist[0, :used] = np.cos(turn)
    twist[1, :used] = -np.sin(turn)
    fine = 2.0 * math.pi / side * (np.arange(side)[:, None] * np.arange(side)[None, :] % side)
    fine_re, fine_im = np.cos(fine), -np.sin(fine)
    fine = np.concatenate([fine_re, fine_im], axis=1)
    twist = np.concatenate([twist[0], twist[1]], axis=1)
    first_high, first_low = split_table(first)
    first = np.concatenate([first_high, first_high, first_low], axis=1)
    blocks = [*split_table(fine), first, *split_table(last), *split_table(twist)]
    wide = max(block.shape[1] for block in blocks)
    stacked = [np.pad(block, ((0, -block.shape[0] % 16), (0, wide - block.shape[1]))) for block in blocks]
    return np.concatenate(stacked, axis=0)


def table_slices(side):
    rows = half_rows(side)
    sizes = ((side, 2 * side),) * 2 + ((2 * rows, 3 * side // 2),) + ((side // 2, 2 * rows),) * 2 + ((rows, 2 * side),) * 2
    starts = np.cumsum([0] + [-(-size[0] // 16) * 16 for size in sizes])
    return [
        (slice(int(start), int(start) + height), slice(0, width))
        for start, (height, width) in zip(starts, sizes)
    ]


def halves(values):
    high = values.astype(jnp.bfloat16)
    low = (values - high.astype(jnp.float32)).astype(jnp.bfloat16)
    return high, low


def matmul(left, right):
    return jnp.dot(left, right, preferred_element_type=jnp.float32)


def gate_kernel(
    query, key_in, value, grad_out, filters, tables,
    sent, inputs, tables_held, taps, sems,
):
    slots, groups, length = query.shape
    per_row = length // LANES
    pairs = [(source, inputs.at[place]) for place, source in enumerate((query, key_in, grad_out, value))]
    pairs += [(filters, taps), (tables, tables_held)]
    copies = [pltpu.make_async_copy(*pair, sems.at[place]) for place, pair in enumerate(pairs)]
    for copy in (copies[5], *copies[:5]):
        copy.start()
    ahead = lax.axis_index("chan")
    products = []
    for first, second in ((0, 1), (2, 3)):
        copies[first].wait()
        copies[second].wait()
        for slot in range(slots):
            products.append(inputs[first, slot].astype(jnp.float32) * inputs[second, slot].astype(jnp.float32))
    pieces = (len(products) + 1) * per_row
    copies[4].wait()
    for which, rows in enumerate((*products, taps[...])):
        rows = pltpu.roll(rows, ahead, 0)
        for part in range(per_row):
            for twin in range(COPIES):
                place = pl.ds(twin * pieces + which * per_row + part, groups, stride=COPIES * pieces)
                sent[place, :] = rows[:, part * LANES : (part + 1) * LANES]
    for copy in copies[5:]:
        copy.wait()


def spectral_kernel(side, parts, signals, combine, got, tables, sent):
    tables_at = table_slices(side)
    fine_high, fine_low, first = [tables[place] for place in tables_at[:3]]
    twist_high, twist_low = [tables[place].astype(jnp.float32) for place in tables_at[5:]]
    twist = twist_high + twist_low
    turn_re, turn_im = twist[:, :side], twist[:, side:]
    mix_high, mix_low = [
        jnp.concatenate([table, jnp.concatenate([-table[:, side:], table[:, :side]], axis=1)], axis=0)
        for table in (fine_high, fine_low)
    ]
    rows = half_rows(side)
    per_row = side // 2 // parts
    pieces = got.shape[0] // parts
    count = parts // COPIES
    mine = per_row * count
    twin = lax.rem(lax.axis_index("seq"), COPIES)
    last_high, last_low = [
        tables[pl.ds(pl.multiple_of(place.start + twin * mine, 16), mine), lanes] for place, lanes in tables_at[3:5]
    ]

    def one(which):
        return jnp.concatenate(
            [got[pl.ds(which * per_row + part, parts, stride=pieces), :] for part in range(per_row)], axis=0
        )

    def turned(real, imag):
        return real * turn_re - imag * turn_im, real * turn_im + imag * turn_re

    def mixed(pairs):
        out = []
        for pair in pairs:
            stack = jnp.concatenate(pair, axis=1)
            high = stack.astype(jnp.bfloat16).astype(jnp.float32)
            both = matmul(jnp.concatenate([high, stack - high], axis=0).astype(jnp.bfloat16), mix_high)
            values = both[:rows] + (both[rows:] + matmul(high.astype(jnp.bfloat16), mix_low))
            out.append((values[:, :side], values[:, side:]))
        return out

    def coarse(which):
        high, low = halves(one(which))
        values = matmul(first, jnp.concatenate([high, low, high], axis=0))
        return turned(values[:rows], values[rows:])

    spectra = mixed([coarse(which) for which in range(signals)])
    products = [turned(*pair) for pair in mixed(combine(*spectra))]
    high, low = halves(
        jnp.concatenate([jnp.concatenate(parts_of, axis=1) for parts_of in zip(*products)], axis=0)
    )
    tall = jnp.concatenate([last_high, last_low], axis=0)
    both = matmul(tall, high)
    result = both[:mine] + (both[mine:] + matmul(last_high, low))
    spread = sent.shape[0] > mine
    for which in range(len(products)):
        for part in range(per_row):
            piece = result[part * count : (part + 1) * count, which * side : (which + 1) * side]
            if spread:
                sent[pl.ds(which * per_row + part, count, stride=pieces), :] = piece
            else:
                sent[pl.ds(part * count, count), :] = piece


def lag_product(*spectra):
    real = imag = 0.0
    half = len(spectra) // 2
    for (gated_re, gated_im), (signal_re, signal_im) in zip(spectra[:half], spectra[half:]):
        real += gated_re * signal_re + gated_im * signal_im
        imag += gated_im * signal_re - gated_re * signal_im
    return [(real, imag)]


def filtered(*spectra):
    half = len(spectra) // 2
    taps_re, taps_im = spectra[-1]
    conv = [(taps_re * re - taps_im * im, -(taps_re * im + taps_im * re)) for re, im in spectra[:half]]
    corr = [(taps_re * re + taps_im * im, taps_im * re - taps_re * im) for re, im in spectra[half:-1]]
    return conv + corr


def pack_kernel(count, rows, lags, sent):
    per_row = lags.shape[0] // count
    pieces = sent.shape[0] // count
    for part in range(per_row):
        sent[pl.ds(pieces - per_row + part, count, stride=pieces), :] = lags[pl.ds(part * count, count), :]


def filter_kernel(spectral, got, tables, skip, sent, gains, sem):
    copy = pltpu.make_async_copy(skip, gains, sem)
    copy.start()
    spectral(got, tables, sent)
    copy.wait()


def grads_kernel(scale, got, inputs, skip, query_grad, key_grad, value_grad, filter_grad):
    _, slots, groups, length = inputs.shape
    per_row = length // LANES
    pieces = (2 * slots + 1) * per_row
    back = lax.rem(groups - lax.axis_index("chan"), groups)
    shape = (groups, groups)
    diagonal = lax.broadcasted_iota(jnp.int32, shape, 0) == lax.broadcasted_iota(jnp.int32, shape, 1)
    for slot in range(slots):
        gains = jnp.broadcast_to(skip[slot : slot + 1, :], shape)
        gain = jnp.sum(jnp.where(diagonal, gains, 0.0), axis=1, keepdims=True)
        for part in range(per_row):
            lanes = slice(part * LANES, (part + 1) * LANES)
            base = slot * per_row + part
            conv = pltpu.roll(got[pl.ds(base, groups, stride=pieces), :], back, 0)
            corr = pltpu.roll(got[pl.ds(base + slots * per_row, groups, stride=pieces), :], back, 0)
            query_f, key_f, cotangent, value_f = [
                inputs[place, slot, :, lanes].astype(jnp.float32) for place in range(4)
            ]
            out_field = conv + gain * (query_f * key_f)
            adjoint = corr + gain * (cotangent * value_f)
            query_grad[slot, :, lanes] = (adjoint * key_f).astype(jnp.bfloat16)
            key_grad[slot, :, lanes] = (adjoint * query_f).astype(jnp.bfloat16)
            value_grad[slot, :, lanes] = (cotangent * out_field).astype(jnp.bfloat16)
    for part in range(per_row):
        lagged = got[pl.ds(2 * slots * per_row + part, groups, stride=pieces), :]
        filter_grad[:, part * LANES : (part + 1) * LANES] = scale * jnp.sum(lagged, axis=0, keepdims=True)


def on_device(kernel, shapes, spaces, scratch=(), aliases=None, out_space=VMEM):
    outs = jax.tree.map(lambda shape: out_space, shapes)
    return pl.pallas_call(
        kernel,
        out_shape=shapes,
        in_specs=spaces,
        out_specs=outs,
        scratch_shapes=scratch,
        input_output_aliases=aliases or {},
        compiler_params=pltpu.CompilerParams(vmem_limit_bytes=LIMIT),
    )


def in_hbm(array):
    return pltpu.with_memory_space_constraint(jnp.asarray(array), pltpu.HBM)


def exchange(rows, axis, count, among=None):
    blocks = rows.reshape(count, 1, rows.size // count)
    return lax.all_to_all(blocks, axis, 0, 0, tiled=True, axis_index_groups=among).reshape(rows.shape)


def local(query, key_in, value, grad_out, filters, skip):
    parts = lax.axis_size("seq")
    chans = lax.axis_size("chan")
    slots, groups, length = query.shape
    total = parts * length
    side = math.isqrt(2 * total)
    pieces = (2 * slots + 1) * length // LANES
    count = parts // COPIES
    packed = jax.ShapeDtypeStruct((parts * pieces, LANES), jnp.float32)
    tables = fourier_tables(side, parts)
    shapes = (
        packed,
        jax.ShapeDtypeStruct((4, *query.shape), query.dtype),
        jax.ShapeDtypeStruct(tables.shape, tables.dtype),
    )
    scratch = [pltpu.VMEM(filters.shape, jnp.float32), pltpu.SemaphoreType.DMA((6,))]
    sent, inputs, tables = on_device(gate_kernel, shapes, [HBM] * 6, scratch)(
        *[in_hbm(array) for array in (query, key_in, value, grad_out, filters, tables)]
    )
    got = exchange(sent, "seq", parts)
    lag_rows = jax.ShapeDtypeStruct((side // 2 // COPIES, LANES), jnp.float32)
    lags = functools.partial(spectral_kernel, side, parts, 2 * slots, lag_product)
    lags = on_device(lags, lag_rows, [VMEM] * 2)(got, tables)
    moves = [
        (s * chans + k, s * chans + (s // COPIES - k) % chans) for s in range(parts) for k in range(chans)
    ]
    lags = lax.ppermute(lags, ("seq", "chan"), moves)
    packed = jax.ShapeDtypeStruct((count * pieces, LANES), jnp.float32)
    rows = functools.partial(spectral_kernel, side, parts, 2 * slots + 1, filtered)
    held = jax.ShapeDtypeStruct(skip.shape, skip.dtype)
    rows = functools.partial(filter_kernel, rows)
    rows, gains = on_device(rows, (packed, held), [VMEM, VMEM, HBM], [pltpu.SemaphoreType.DMA])(
        got, tables, in_hbm(skip)
    )
    sent = on_device(functools.partial(pack_kernel, count), packed, [VMEM] * 2, aliases={0: 0})(rows, lags)
    got = exchange(sent, "seq", count, [list(range(twin, parts, COPIES)) for twin in range(COPIES)])
    grad = jax.ShapeDtypeStruct(query.shape, jnp.bfloat16)
    row = jax.ShapeDtypeStruct((1, length), jnp.float32)
    scale = 1.0 / math.sqrt(slots * chans * total)
    grads = functools.partial(grads_kernel, scale)
    return on_device(grads, (grad, grad, grad, row), [VMEM] * 3)(got, inputs, gains)


def solution(mesh):
    spread = P("chan", None, "seq")
    return jax.shard_map(
        local,
        mesh=mesh,
        in_specs=(spread, spread, spread, spread, P(None, "seq"), P("chan", None)),
        out_specs=(spread, spread, spread, P("chan", "seq")),
        check_vma=False,
    )
```

```python
import functools
import math

import jax
import jax.numpy as jnp
import ml_dtypes
import numpy as np
from jax import lax
from jax.experimental import pallas as pl
from jax.experimental.pallas import tpu as pltpu
from jax.sharding import PartitionSpec as P

LANES = 128
VMEM = pl.BlockSpec(memory_space=pltpu.VMEM)
HBM = pl.BlockSpec(memory_space=pltpu.HBM)
LIMIT = 16 * 1024 * 1024
COPIES = 2


def split_table(table):
    high = table.astype(ml_dtypes.bfloat16)
    low = (table - high.astype(np.float64)).astype(ml_dtypes.bfloat16)
    return high, low


def half_rows(side):
    return -(-(side // 2 + 1) // 8) * 8


def fourier_tables(side, parts):
    used = side // 2 + 1
    rows = half_rows(side)
    per_block = side // 2 // parts
    order = np.arange(side // 2).reshape(parts, per_block).T.reshape(-1)
    coarse = np.arange(used)
    angle = 2.0 * math.pi / side * (coarse[:, None] * order[None, :] % side)
    first = np.zeros((2, rows, side // 2))
    first[0, :used] = np.cos(angle)
    first[1, :used] = -np.sin(angle)
    first = first.reshape(2 * rows, side // 2)
    weight = np.full((used,), 2.0)
    weight[0] = weight[-1] = 1.0
    last = np.zeros((side // 2, 2, rows))
    last[:, 0, :used] = (weight[:, None] * np.cos(angle)).T / side**2
    last[:, 1, :used] = (weight[:, None] * np.sin(angle)).T / side**2
    last = last.reshape(per_block, parts // COPIES, COPIES, 2 * rows)
    last = last.transpose(2, 0, 1, 3).reshape(side // 2, 2 * rows)
    turn = 2.0 * math.pi / side**2 * (coarse[:, None] * np.arange(side)[None, :])
    twist = np.zeros((2, rows, side))
    twist[0, :used] = np.cos(turn)
    twist[1, :used] = -np.sin(turn)
    fine = 2.0 * math.pi / side * (np.arange(side)[:, None] * np.arange(side)[None, :] % side)
    fine_re, fine_im = np.cos(fine), -np.sin(fine)
    fine = np.concatenate([fine_re, fine_im], axis=1)
    twist = np.concatenate([twist[0], twist[1]], axis=1)
    first_high, first_low = split_table(first)
    first = np.concatenate([first_high, first_high, first_low], axis=1)
    blocks = [*split_table(fine), first, *split_table(last), *split_table(twist)]
    wide = max(block.shape[1] for block in blocks)
    stacked = [np.pad(block, ((0, -block.shape[0] % 16), (0, wide - block.shape[1]))) for block in blocks]
    return np.concatenate(stacked, axis=0)


def table_slices(side):
    rows = half_rows(side)
    sizes = ((side, 2 * side),) * 2 + ((2 * rows, 3 * side // 2),) + ((side // 2, 2 * rows),) * 2 + ((rows, 2 * side),) * 2
    starts = np.cumsum([0] + [-(-size[0] // 16) * 16 for size in sizes])
    return [
        (slice(int(start), int(start) + height), slice(0, width))
        for start, (height, width) in zip(starts, sizes)
    ]


def halves(values):
    high = values.astype(jnp.bfloat16)
    low = (values - high.astype(jnp.float32)).astype(jnp.bfloat16)
    return high, low


def matmul(left, right):
    return jnp.dot(left, right, preferred_element_type=jnp.float32)


def gate_kernel(
    query, key_in, value, grad_out, filters, tables,
    sent, inputs, tables_held, taps, sems,
):
    slots, groups, length = query.shape
    per_row = length // LANES
    pairs = [(source, inputs.at[place]) for place, source in enumerate((query, key_in, grad_out, value))]
    pairs += [(filters, taps), (tables, tables_held)]
    copies = [pltpu.make_async_copy(*pair, sems.at[place]) for place, pair in enumerate(pairs)]
    for copy in (copies[5], *copies[:5]):
        copy.start()
    ahead = lax.axis_index("chan")
    products = []
    for first, second in ((0, 1), (2, 3)):
        copies[first].wait()
        copies[second].wait()
        for slot in range(slots):
            products.append(inputs[first, slot].astype(jnp.float32) * inputs[second, slot].astype(jnp.float32))
    pieces = (len(products) + 1) * per_row
    copies[4].wait()
    for which, rows in enumerate((*products, taps[...])):
        rows = pltpu.roll(rows, ahead, 0)
        for part in range(per_row):
            for twin in range(COPIES):
                place = pl.ds(twin * pieces + which * per_row + part, groups, stride=COPIES * pieces)
                sent[place, :] = rows[:, part * LANES : (part + 1) * LANES]
    for copy in copies[5:]:
        copy.wait()


def spectral_kernel(side, parts, signals, combine, got, tables, sent):
    tables_at = table_slices(side)
    fine_high, fine_low, first = [tables[place] for place in tables_at[:3]]
    twist_high, twist_low = [tables[place].astype(jnp.float32) for place in tables_at[5:]]
    twist = twist_high + twist_low
    turn_re, turn_im = twist[:, :side], twist[:, side:]
    mix_high, mix_low = [
        jnp.concatenate([table, jnp.concatenate([-table[:, side:], table[:, :side]], axis=1)], axis=0)
        for table in (fine_high, fine_low)
    ]
    rows = half_rows(side)
    per_row = side // 2 // parts
    pieces = got.shape[0] // parts
    count = parts // COPIES
    mine = per_row * count
    twin = lax.rem(lax.axis_index("seq"), COPIES)
    last_high, last_low = [
        tables[pl.ds(pl.multiple_of(place.start + twin * mine, 16), mine), lanes] for place, lanes in tables_at[3:5]
    ]

    def one(which):
        return jnp.concatenate(
            [got[pl.ds(which * per_row + part, parts, stride=pieces), :] for part in range(per_row)], axis=0
        )

    def turned(real, imag):
        return real * turn_re - imag * turn_im, real * turn_im + imag * turn_re

    def mixed(pairs):
        out = []
        for pair in pairs:
            stack = jnp.concatenate(pair, axis=1)
            high = stack.astype(jnp.bfloat16).astype(jnp.float32)
            both = matmul(jnp.concatenate([high, stack - high], axis=0).astype(jnp.bfloat16), mix_high)
            values = both[:rows] + (both[rows:] + matmul(high.astype(jnp.bfloat16), mix_low))
            out.append((values[:, :side], values[:, side:]))
        return out

    def coarse(which):
        high, low = halves(one(which))
        values = matmul(first, jnp.concatenate([high, low, high], axis=0))
        return turned(values[:rows], values[rows:])

    spectra = mixed([coarse(which) for which in range(signals)])
    products = [turned(*pair) for pair in mixed(combine(*spectra))]
    high, low = halves(
        jnp.concatenate([jnp.concatenate(parts_of, axis=1) for parts_of in zip(*products)], axis=0)
    )
    tall = jnp.concatenate([last_high, last_low], axis=0)
    both = matmul(tall, high)
    result = both[:mine] + (both[mine:] + matmul(last_high, low))
    spread = sent.shape[0] > mine
    for which in range(len(products)):
        for part in range(per_row):
            piece = result[part * count : (part + 1) * count, which * side : (which + 1) * side]
            if spread:
                sent[pl.ds(which * per_row + part, count, stride=pieces), :] = piece
            else:
                sent[pl.ds(part * count, count), :] = piece


def lag_product(*spectra):
    real = imag = 0.0
    half = len(spectra) // 2
    for (gated_re, gated_im), (signal_re, signal_im) in zip(spectra[:half], spectra[half:]):
        real += gated_re * signal_re + gated_im * signal_im
        imag += gated_im * signal_re - gated_re * signal_im
    return [(real, imag)]


def filtered(*spectra):
    half = len(spectra) // 2
    taps_re, taps_im = spectra[-1]
    conv = [(taps_re * re - taps_im * im, -(taps_re * im + taps_im * re)) for re, im in spectra[:half]]
    corr = [(taps_re * re + taps_im * im, taps_im * re - taps_re * im) for re, im in spectra[half:-1]]
    return conv + corr


def pack_kernel(count, rows, lags, sent):
    per_row = lags.shape[0] // count
    pieces = sent.shape[0] // count
    for part in range(per_row):
        sent[pl.ds(pieces - per_row + part, count, stride=pieces), :] = lags[pl.ds(part * count, count), :]


def filter_kernel(spectral, got, tables, skip, sent, gains, fetched, sem):
    copy = pltpu.make_async_copy(skip, fetched, sem)
    copy.start()
    spectral(got, tables, sent)
    copy.wait()
    slots, groups, _ = gains.shape
    shape = (groups, groups)
    diagonal = lax.broadcasted_iota(jnp.int32, shape, 0) == lax.broadcasted_iota(jnp.int32, shape, 1)
    for slot in range(slots):
        spread = jnp.broadcast_to(fetched[slot : slot + 1, :], shape)
        gain = jnp.sum(jnp.where(diagonal, spread, 0.0), axis=1, keepdims=True)
        gains[slot] = jnp.broadcast_to(gain, gains.shape[1:])


def grads_kernel(scale, got, inputs, gains, query_grad, key_grad, value_grad, filter_grad):
    _, slots, groups, length = inputs.shape
    per_row = length // LANES
    pieces = (2 * slots + 1) * per_row
    back = lax.rem(groups - lax.axis_index("chan"), groups)
    for slot in range(slots):
        gain = gains[slot]
        for part in range(per_row):
            lanes = slice(part * LANES, (part + 1) * LANES)
            base = slot * per_row + part
            conv = pltpu.roll(got[pl.ds(base, groups, stride=pieces), :], back, 0)
            corr = pltpu.roll(got[pl.ds(base + slots * per_row, groups, stride=pieces), :], back, 0)
            query_f, key_f, cotangent, value_f = [
                inputs[place, slot, :, lanes].astype(jnp.float32) for place in range(4)
            ]
            out_field = conv + gain * (query_f * key_f)
            adjoint = corr + gain * (cotangent * value_f)
            query_grad[slot, :, lanes] = (adjoint * key_f).astype(jnp.bfloat16)
            key_grad[slot, :, lanes] = (adjoint * query_f).astype(jnp.bfloat16)
            value_grad[slot, :, lanes] = (cotangent * out_field).astype(jnp.bfloat16)
    for part in range(per_row):
        lagged = got[pl.ds(2 * slots * per_row + part, groups, stride=pieces), :]
        filter_grad[:, part * LANES : (part + 1) * LANES] = scale * jnp.sum(lagged, axis=0, keepdims=True)


def on_device(kernel, shapes, spaces, scratch=(), aliases=None, out_space=VMEM):
    outs = jax.tree.map(lambda shape: out_space, shapes)
    return pl.pallas_call(
        kernel,
        out_shape=shapes,
        in_specs=spaces,
        out_specs=outs,
        scratch_shapes=scratch,
        input_output_aliases=aliases or {},
        compiler_params=pltpu.CompilerParams(vmem_limit_bytes=LIMIT),
    )


def in_hbm(array):
    return pltpu.with_memory_space_constraint(jnp.asarray(array), pltpu.HBM)


def exchange(rows, axis, count, among=None):
    blocks = rows.reshape(count, 1, rows.size // count)
    return lax.all_to_all(blocks, axis, 0, 0, tiled=True, axis_index_groups=among).reshape(rows.shape)


def local(query, key_in, value, grad_out, filters, skip):
    parts = lax.axis_size("seq")
    chans = lax.axis_size("chan")
    slots, groups, length = query.shape
    total = parts * length
    side = math.isqrt(2 * total)
    pieces = (2 * slots + 1) * length // LANES
    count = parts // COPIES
    packed = jax.ShapeDtypeStruct((parts * pieces, LANES), jnp.float32)
    tables = fourier_tables(side, parts)
    shapes = (
        packed,
        jax.ShapeDtypeStruct((4, *query.shape), query.dtype),
        jax.ShapeDtypeStruct(tables.shape, tables.dtype),
    )
    scratch = [pltpu.VMEM(filters.shape, jnp.float32), pltpu.SemaphoreType.DMA((6,))]
    sent, inputs, tables = on_device(gate_kernel, shapes, [HBM] * 6, scratch)(
        *[in_hbm(array) for array in (query, key_in, value, grad_out, filters, tables)]
    )
    got = exchange(sent, "seq", parts)
    lag_rows = jax.ShapeDtypeStruct((side // 2 // COPIES, LANES), jnp.float32)
    lags = functools.partial(spectral_kernel, side, parts, 2 * slots, lag_product)
    lags = on_device(lags, lag_rows, [VMEM] * 2)(got, tables)
    moves = [
        (s * chans + k, s * chans + (s // COPIES - k) % chans) for s in range(parts) for k in range(chans)
    ]
    lags = lax.ppermute(lags, ("seq", "chan"), moves)
    packed = jax.ShapeDtypeStruct((count * pieces, LANES), jnp.float32)
    rows = functools.partial(spectral_kernel, side, parts, 2 * slots + 1, filtered)
    held = jax.ShapeDtypeStruct((*skip.shape, LANES), jnp.float32)
    scratch = [pltpu.VMEM(skip.shape, jnp.float32), pltpu.SemaphoreType.DMA]
    rows = functools.partial(filter_kernel, rows)
    rows, gains = on_device(rows, (packed, held), [VMEM, VMEM, HBM], scratch)(
        got, tables, in_hbm(skip)
    )
    sent = on_device(functools.partial(pack_kernel, count), packed, [VMEM] * 2, aliases={0: 0})(rows, lags)
    got = exchange(sent, "seq", count, [list(range(twin, parts, COPIES)) for twin in range(COPIES)])
    grad = jax.ShapeDtypeStruct(query.shape, jnp.bfloat16)
    row = jax.ShapeDtypeStruct((1, length), jnp.float32)
    scale = 1.0 / math.sqrt(slots * chans * total)
    grads = functools.partial(grads_kernel, scale)
    return on_device(grads, (grad, grad, grad, row), [VMEM] * 3)(got, inputs, gains)


def solution(mesh):
    spread = P("chan", None, "seq")
    return jax.shard_map(
        local,
        mesh=mesh,
        in_specs=(spread, spread, spread, spread, P(None, "seq"), P("chan", None)),
        out_specs=(spread, spread, spread, P("chan", "seq")),
        check_vma=False,
    )
```

```python
import functools
import math

import jax
import jax.numpy as jnp
import ml_dtypes
import numpy as np
from jax import lax
from jax.experimental import pallas as pl
from jax.experimental.pallas import tpu as pltpu
from jax.sharding import PartitionSpec as P

LANES = 128
VMEM = pl.BlockSpec(memory_space=pltpu.VMEM)
HBM = pl.BlockSpec(memory_space=pltpu.HBM)
LIMIT = 16 * 1024 * 1024
COPIES = 2


def split_table(table):
    high = table.astype(ml_dtypes.bfloat16)
    low = (table - high.astype(np.float64)).astype(ml_dtypes.bfloat16)
    return high, low


def half_rows(side):
    return -(-(side // 2 + 1) // 8) * 8


def fourier_tables(side, parts):
    used = side // 2 + 1
    rows = half_rows(side)
    per_block = side // 2 // parts
    order = np.arange(side // 2).reshape(parts, per_block).T.reshape(-1)
    coarse = np.arange(used)
    angle = 2.0 * math.pi / side * (coarse[:, None] * order[None, :] % side)
    first = np.zeros((2, rows, side // 2))
    first[0, :used] = np.cos(angle)
    first[1, :used] = -np.sin(angle)
    first = first.reshape(2 * rows, side // 2)
    weight = np.full((used,), 2.0)
    weight[0] = weight[-1] = 1.0
    last = np.zeros((side // 2, 2, rows))
    last[:, 0, :used] = (weight[:, None] * np.cos(angle)).T / side**2
    last[:, 1, :used] = (weight[:, None] * np.sin(angle)).T / side**2
    last = last.reshape(per_block, parts // COPIES, COPIES, 2 * rows)
    last = last.transpose(2, 0, 1, 3).reshape(side // 2, 2 * rows)
    turn = 2.0 * math.pi / side**2 * (coarse[:, None] * np.arange(side)[None, :])
    twist = np.zeros((2, rows, side))
    twist[0, :used] = np.cos(turn)
    twist[1, :used] = -np.sin(turn)
    fine = 2.0 * math.pi / side * (np.arange(side)[:, None] * np.arange(side)[None, :] % side)
    fine_re, fine_im = np.cos(fine), -np.sin(fine)
    fine = np.concatenate([fine_re, fine_im], axis=1)
    twist = np.concatenate([twist[0], twist[1]], axis=1)
    first_high, first_low = split_table(first)
    first = np.concatenate([first_high, first_high, first_low], axis=1)
    fine, last, twist = [np.concatenate(split_table(table), axis=0) for table in (fine, last, twist)]
    return fine, first, last, twist


def halves(values):
    high = values.astype(jnp.bfloat16)
    low = (values - high.astype(jnp.float32)).astype(jnp.bfloat16)
    return high, low


def matmul(left, right):
    return jnp.dot(left, right, preferred_element_type=jnp.float32)


def gate_kernel(
    query, key_in, value, grad_out, filters,
    sent, inputs, taps, sems,
):
    slots, groups, length = query.shape
    per_row = length // LANES
    pairs = [(source, inputs.at[place]) for place, source in enumerate((query, key_in, grad_out, value))]
    pairs += [(filters, taps)]
    copies = [pltpu.make_async_copy(*pair, sems.at[place]) for place, pair in enumerate(pairs)]
    for copy in copies:
        copy.start()
    ahead = lax.axis_index("chan")
    products = []
    for first, second in ((0, 1), (2, 3)):
        copies[first].wait()
        copies[second].wait()
        for slot in range(slots):
            products.append(inputs[first, slot].astype(jnp.float32) * inputs[second, slot].astype(jnp.float32))
    pieces = (len(products) + 1) * per_row
    copies[4].wait()
    for which, rows in enumerate((*products, taps[...])):
        rows = pltpu.roll(rows, ahead, 0)
        for part in range(per_row):
            for twin in range(COPIES):
                place = pl.ds(twin * pieces + which * per_row + part, groups, stride=COPIES * pieces)
                sent[place, :] = rows[:, part * LANES : (part + 1) * LANES]


def spectral_kernel(side, parts, signals, combine, got, fine, first, last, twist, sent):
    fine_high, fine_low = fine[:side], fine[side:]
    first = first[...]
    rows = half_rows(side)
    twist = twist[...].astype(jnp.float32)
    twist = twist[:rows] + twist[rows:]
    turn_re, turn_im = twist[:, :side], twist[:, side:]
    mix_high, mix_low = [
        jnp.concatenate([table, jnp.concatenate([-table[:, side:], table[:, :side]], axis=1)], axis=0)
        for table in (fine_high, fine_low)
    ]
    rows = half_rows(side)
    per_row = side // 2 // parts
    pieces = got.shape[0] // parts
    count = parts // COPIES
    mine = per_row * count
    twin = lax.rem(lax.axis_index("seq"), COPIES)
    start = pl.multiple_of(twin * mine, 16)
    last_high, last_low = last[pl.ds(start, mine), :], last[pl.ds(side // 2 + start, mine), :]

    def one(which):
        return jnp.concatenate(
            [got[pl.ds(which * per_row + part, parts, stride=pieces), :] for part in range(per_row)], axis=0
        )

    def turned(real, imag):
        return real * turn_re - imag * turn_im, real * turn_im + imag * turn_re

    def mixed(pairs):
        out = []
        for pair in pairs:
            stack = jnp.concatenate(pair, axis=1)
            high = stack.astype(jnp.bfloat16).astype(jnp.float32)
            both = matmul(jnp.concatenate([high, stack - high], axis=0).astype(jnp.bfloat16), mix_high)
            values = both[:rows] + (both[rows:] + matmul(high.astype(jnp.bfloat16), mix_low))
            out.append((values[:, :side], values[:, side:]))
        return out

    def coarse(which):
        high, low = halves(one(which))
        values = matmul(first, jnp.concatenate([high, low, high], axis=0))
        return turned(values[:rows], values[rows:])

    spectra = mixed([coarse(which) for which in range(signals)])
    products = [turned(*pair) for pair in mixed(combine(*spectra))]
    high, low = halves(
        jnp.concatenate([jnp.concatenate(parts_of, axis=1) for parts_of in zip(*products)], axis=0)
    )
    tall = jnp.concatenate([last_high, last_low], axis=0)
    both = matmul(tall, high)
    result = both[:mine] + (both[mine:] + matmul(last_high, low))
    spread = sent.shape[0] > mine
    for which in range(len(products)):
        for part in range(per_row):
            piece = result[part * count : (part + 1) * count, which * side : (which + 1) * side]
            if spread:
                sent[pl.ds(which * per_row + part, count, stride=pieces), :] = piece
            else:
                sent[pl.ds(part * count, count), :] = piece


def lag_product(*spectra):
    real = imag = 0.0
    half = len(spectra) // 2
    for (gated_re, gated_im), (signal_re, signal_im) in zip(spectra[:half], spectra[half:]):
        real += gated_re * signal_re + gated_im * signal_im
        imag += gated_im * signal_re - gated_re * signal_im
    return [(real, imag)]


def filtered(*spectra):
    half = len(spectra) // 2
    taps_re, taps_im = spectra[-1]
    conv = [(taps_re * re - taps_im * im, -(taps_re * im + taps_im * re)) for re, im in spectra[:half]]
    corr = [(taps_re * re + taps_im * im, taps_im * re - taps_re * im) for re, im in spectra[half:-1]]
    return conv + corr


def pack_kernel(count, rows, lags, sent):
    per_row = lags.shape[0] // count
    pieces = sent.shape[0] // count
    for part in range(per_row):
        sent[pl.ds(pieces - per_row + part, count, stride=pieces), :] = lags[pl.ds(part * count, count), :]


def filter_kernel(spectral, got, fine, first, last, twist, skip, sent, gains, fetched, sem):
    copy = pltpu.make_async_copy(skip, fetched, sem)
    copy.start()
    spectral(got, fine, first, last, twist, sent)
    copy.wait()
    slots, groups, _ = gains.shape
    shape = (groups, groups)
    diagonal = lax.broadcasted_iota(jnp.int32, shape, 0) == lax.broadcasted_iota(jnp.int32, shape, 1)
    for slot in range(slots):
        spread = jnp.broadcast_to(fetched[slot : slot + 1, :], shape)
        gain = jnp.sum(jnp.where(diagonal, spread, 0.0), axis=1, keepdims=True)
        gains[slot] = jnp.broadcast_to(gain, gains.shape[1:])


def grads_kernel(scale, got, inputs, gains, query_grad, key_grad, value_grad, filter_grad):
    _, slots, groups, length = inputs.shape
    per_row = length // LANES
    pieces = (2 * slots + 1) * per_row
    back = lax.rem(groups - lax.axis_index("chan"), groups)
    for slot in range(slots):
        gain = gains[slot]
        for part in range(per_row):
            lanes = slice(part * LANES, (part + 1) * LANES)
            base = slot * per_row + part
            conv = pltpu.roll(got[pl.ds(base, groups, stride=pieces), :], back, 0)
            corr = pltpu.roll(got[pl.ds(base + slots * per_row, groups, stride=pieces), :], back, 0)
            query_f, key_f, cotangent, value_f = [
                inputs[place, slot, :, lanes].astype(jnp.float32) for place in range(4)
            ]
            out_field = conv + gain * (query_f * key_f)
            adjoint = corr + gain * (cotangent * value_f)
            query_grad[slot, :, lanes] = (adjoint * key_f).astype(jnp.bfloat16)
            key_grad[slot, :, lanes] = (adjoint * query_f).astype(jnp.bfloat16)
            value_grad[slot, :, lanes] = (cotangent * out_field).astype(jnp.bfloat16)
    for part in range(per_row):
        lagged = got[pl.ds(2 * slots * per_row + part, groups, stride=pieces), :]
        filter_grad[:, part * LANES : (part + 1) * LANES] = scale * jnp.sum(lagged, axis=0, keepdims=True)


def on_device(kernel, shapes, spaces, scratch=(), aliases=None, out_space=VMEM):
    outs = jax.tree.map(lambda shape: out_space, shapes)
    return pl.pallas_call(
        kernel,
        out_shape=shapes,
        in_specs=spaces,
        out_specs=outs,
        scratch_shapes=scratch,
        input_output_aliases=aliases or {},
        compiler_params=pltpu.CompilerParams(vmem_limit_bytes=LIMIT),
    )


def in_hbm(array):
    return pltpu.with_memory_space_constraint(jnp.asarray(array), pltpu.HBM)


def exchange(rows, axis, count, among=None):
    blocks = rows.reshape(count, 1, rows.size // count)
    return lax.all_to_all(blocks, axis, 0, 0, tiled=True, axis_index_groups=among).reshape(rows.shape)


def local(query, key_in, value, grad_out, filters, skip):
    parts = lax.axis_size("seq")
    chans = lax.axis_size("chan")
    slots, groups, length = query.shape
    total = parts * length
    side = math.isqrt(2 * total)
    pieces = (2 * slots + 1) * length // LANES
    count = parts // COPIES
    packed = jax.ShapeDtypeStruct((parts * pieces, LANES), jnp.float32)
    tables = fourier_tables(side, parts)
    shapes = (
        packed,
        jax.ShapeDtypeStruct((4, *query.shape), query.dtype),
    )
    scratch = [pltpu.VMEM(filters.shape, jnp.float32), pltpu.SemaphoreType.DMA((5,))]
    sent, inputs = on_device(gate_kernel, shapes, [HBM] * 5, scratch)(
        *[in_hbm(array) for array in (query, key_in, value, grad_out, filters)]
    )
    got = exchange(sent, "seq", parts)
    lag_rows = jax.ShapeDtypeStruct((side // 2 // COPIES, LANES), jnp.float32)
    lags = functools.partial(spectral_kernel, side, parts, 2 * slots, lag_product)
    lags = on_device(lags, lag_rows, [VMEM] * 5)(got, *tables)
    moves = [
        (s * chans + k, s * chans + (s // COPIES - k) % chans) for s in range(parts) for k in range(chans)
    ]
    lags = lax.ppermute(lags, ("seq", "chan"), moves)
    packed = jax.ShapeDtypeStruct((count * pieces, LANES), jnp.float32)
    rows = functools.partial(spectral_kernel, side, parts, 2 * slots + 1, filtered)
    held = jax.ShapeDtypeStruct((*skip.shape, LANES), jnp.float32)
    scratch = [pltpu.VMEM(skip.shape, jnp.float32), pltpu.SemaphoreType.DMA]
    rows = functools.partial(filter_kernel, rows)
    rows, gains = on_device(rows, (packed, held), [*[VMEM] * 5, HBM], scratch)(
        got, *tables, in_hbm(skip)
    )
    sent = on_device(functools.partial(pack_kernel, count), packed, [VMEM] * 2, aliases={0: 0})(rows, lags)
    got = exchange(sent, "seq", count, [list(range(twin, parts, COPIES)) for twin in range(COPIES)])
    grad = jax.ShapeDtypeStruct(query.shape, jnp.bfloat16)
    row = jax.ShapeDtypeStruct((1, length), jnp.float32)
    scale = 1.0 / math.sqrt(slots * chans * total)
    grads = functools.partial(grads_kernel, scale)
    return on_device(grads, (grad, grad, grad, row), [VMEM] * 3)(got, inputs, gains)


def solution(mesh):
    spread = P("chan", None, "seq")
    return jax.shard_map(
        local,
        mesh=mesh,
        in_specs=(spread, spread, spread, spread, P(None, "seq"), P("chan", None)),
        out_specs=(spread, spread, spread, P("chan", "seq")),
        check_vma=False,
    )
```

```python
import functools
import math

import jax
import jax.numpy as jnp
import ml_dtypes
import numpy as np
from jax import lax
from jax.experimental import pallas as pl
from jax.experimental.pallas import tpu as pltpu
from jax.sharding import PartitionSpec as P

LANES = 128
VMEM = pl.BlockSpec(memory_space=pltpu.VMEM)
HBM = pl.BlockSpec(memory_space=pltpu.HBM)
LIMIT = 16 * 1024 * 1024
COPIES = 2


def split_table(table):
    high = table.astype(ml_dtypes.bfloat16)
    low = (table - high.astype(np.float64)).astype(ml_dtypes.bfloat16)
    return high, low


def half_rows(side):
    return -(-(side // 2 + 1) // 8) * 8


def fourier_tables(side, parts):
    used = side // 2 + 1
    rows = half_rows(side)
    per_block = side // 2 // parts
    order = np.arange(side // 2).reshape(parts, per_block).T.reshape(-1)
    coarse = np.arange(used)
    angle = 2.0 * math.pi / side * (coarse[:, None] * order[None, :] % side)
    first = np.zeros((2, rows, side // 2))
    first[0, :used] = np.cos(angle)
    first[1, :used] = -np.sin(angle)
    first = first.reshape(2 * rows, side // 2)
    weight = np.full((used,), 2.0)
    weight[0] = weight[-1] = 1.0
    last = np.zeros((side // 2, 2, rows))
    last[:, 0, :used] = (weight[:, None] * np.cos(angle)).T / side**2
    last[:, 1, :used] = (weight[:, None] * np.sin(angle)).T / side**2
    last = last.reshape(per_block, parts // COPIES, COPIES, 2 * rows)
    last = last.transpose(2, 0, 1, 3).reshape(side // 2, 2 * rows)
    turn = 2.0 * math.pi / side**2 * (coarse[:, None] * np.arange(side)[None, :])
    twist = np.zeros((2, rows, side))
    twist[0, :used] = np.cos(turn)
    twist[1, :used] = -np.sin(turn)
    fine = 2.0 * math.pi / side * (np.arange(side)[:, None] * np.arange(side)[None, :] % side)
    fine_re, fine_im = np.cos(fine), -np.sin(fine)
    fine = np.concatenate([fine_re, fine_im], axis=1)
    twist = np.concatenate([twist[0], twist[1]], axis=1)
    first_high, first_low = split_table(first)
    first = np.concatenate([first_high, first_high, first_low], axis=1)
    fine, last, twist = [np.concatenate(split_table(table), axis=0) for table in (fine, last, twist)]
    return fine, first, last, twist


def halves(values):
    high = values.astype(jnp.bfloat16)
    low = (values - high.astype(jnp.float32)).astype(jnp.bfloat16)
    return high, low


def matmul(left, right):
    return jnp.dot(left, right, preferred_element_type=jnp.float32)


def gate_kernel(
    query, key_in, value, grad_out, filters,
    sent, inputs, taps, sems,
):
    slots, groups, length = query.shape
    per_row = length // LANES
    pairs = [(source, inputs.at[place]) for place, source in enumerate((query, key_in, grad_out, value))]
    pairs += [(filters, taps)]
    copies = [pltpu.make_async_copy(*pair, sems.at[place]) for place, pair in enumerate(pairs)]
    for copy in copies:
        copy.start()
    ahead = lax.axis_index("chan")
    products = []
    for first, second in ((0, 1), (2, 3)):
        copies[first].wait()
        copies[second].wait()
        for slot in range(slots):
            products.append(inputs[first, slot].astype(jnp.float32) * inputs[second, slot].astype(jnp.float32))
    pieces = (len(products) + 1) * per_row
    copies[4].wait()
    for which, rows in enumerate((*products, taps[...])):
        rows = pltpu.roll(rows, ahead, 0)
        for part in range(per_row):
            for twin in range(COPIES):
                place = pl.ds(twin * pieces + which * per_row + part, groups, stride=COPIES * pieces)
                sent[place, :] = rows[:, part * LANES : (part + 1) * LANES]


def spectral_kernel(side, parts, signals, combine, got, fine, first, last, twist, sent):
    fine_high, fine_low = fine[:side], fine[side:]
    first = first[...]
    rows = half_rows(side)
    twist = twist[...].astype(jnp.float32)
    twist = twist[:rows] + twist[rows:]
    turn_re, turn_im = twist[:, :side], twist[:, side:]
    mix_high, mix_low = [
        jnp.concatenate([table, jnp.concatenate([-table[:, side:], table[:, :side]], axis=1)], axis=0)
        for table in (fine_high, fine_low)
    ]
    rows = half_rows(side)
    per_row = side // 2 // parts
    pieces = got.shape[0] // parts
    count = parts // COPIES
    mine = per_row * count
    twin = lax.rem(lax.axis_index("seq"), COPIES)
    start = pl.multiple_of(twin * mine, 16)
    last_high, last_low = last[pl.ds(start, mine), :], last[pl.ds(side // 2 + start, mine), :]

    def one(which):
        return jnp.concatenate(
            [got[pl.ds(which * per_row + part, parts, stride=pieces), :] for part in range(per_row)], axis=0
        )

    def turned(real, imag):
        return real * turn_re - imag * turn_im, real * turn_im + imag * turn_re

    def mixed(pairs):
        out = []
        for pair in pairs:
            stack = jnp.concatenate(pair, axis=1)
            high = stack.astype(jnp.bfloat16).astype(jnp.float32)
            both = matmul(jnp.concatenate([high, stack - high], axis=0).astype(jnp.bfloat16), mix_high)
            values = both[:rows] + (both[rows:] + matmul(high.astype(jnp.bfloat16), mix_low))
            out.append((values[:, :side], values[:, side:]))
        return out

    def coarse(which):
        high, low = halves(one(which))
        values = matmul(first, jnp.concatenate([high, low, high], axis=0))
        return turned(values[:rows], values[rows:])

    spectra = mixed([coarse(which) for which in range(signals)])
    products = [turned(*pair) for pair in mixed(combine(*spectra))]
    high, low = halves(
        jnp.concatenate([jnp.concatenate(parts_of, axis=1) for parts_of in zip(*products)], axis=0)
    )
    tall = jnp.concatenate([last_high, last_low], axis=0)
    both = matmul(tall, high)
    result = both[:mine] + (both[mine:] + matmul(last_high, low))
    spread = sent.shape[0] > mine
    for which in range(len(products)):
        for part in range(per_row):
            piece = result[part * count : (part + 1) * count, which * side : (which + 1) * side]
            if spread:
                sent[pl.ds(which * per_row + part, count, stride=pieces), :] = piece
            else:
                sent[pl.ds(part * count, count), :] = piece


def lag_product(*spectra):
    real = imag = 0.0
    half = len(spectra) // 2
    for (gated_re, gated_im), (signal_re, signal_im) in zip(spectra[:half], spectra[half:]):
        real += gated_re * signal_re + gated_im * signal_im
        imag += gated_im * signal_re - gated_re * signal_im
    return [(real, imag)]


def filtered(*spectra):
    half = len(spectra) // 2
    taps_re, taps_im = spectra[-1]
    conv = [(taps_re * re - taps_im * im, -(taps_re * im + taps_im * re)) for re, im in spectra[:half]]
    corr = [(taps_re * re + taps_im * im, taps_im * re - taps_re * im) for re, im in spectra[half:-1]]
    return conv + corr


def pack_kernel(count, rows, lags, sent):
    per_row = lags.shape[0] // count
    pieces = sent.shape[0] // count
    for part in range(per_row):
        sent[pl.ds(pieces - per_row + part, count, stride=pieces), :] = lags[pl.ds(part * count, count), :]


def filter_kernel(spectral, got, fine, first, last, twist, skip, sent, gains, sem):
    copy = pltpu.make_async_copy(skip, gains, sem)
    copy.start()
    spectral(got, fine, first, last, twist, sent)
    copy.wait()


def grads_kernel(scale, got, inputs, skip, query_grad, key_grad, value_grad, filter_grad):
    _, slots, groups, length = inputs.shape
    per_row = length // LANES
    pieces = (2 * slots + 1) * per_row
    back = lax.rem(groups - lax.axis_index("chan"), groups)
    shape = (groups, groups)
    diagonal = lax.broadcasted_iota(jnp.int32, shape, 0) == lax.broadcasted_iota(jnp.int32, shape, 1)
    for slot in range(slots):
        gains = jnp.broadcast_to(skip[slot : slot + 1, :], shape)
        gain = jnp.sum(jnp.where(diagonal, gains, 0.0), axis=1, keepdims=True)
        for part in range(per_row):
            lanes = slice(part * LANES, (part + 1) * LANES)
            base = slot * per_row + part
            conv = pltpu.roll(got[pl.ds(base, groups, stride=pieces), :], back, 0)
            corr = pltpu.roll(got[pl.ds(base + slots * per_row, groups, stride=pieces), :], back, 0)
            query_f, key_f, cotangent, value_f = [
                inputs[place, slot, :, lanes].astype(jnp.float32) for place in range(4)
            ]
            out_field = conv + gain * (query_f * key_f)
            adjoint = corr + gain * (cotangent * value_f)
            query_grad[slot, :, lanes] = (adjoint * key_f).astype(jnp.bfloat16)
            key_grad[slot, :, lanes] = (adjoint * query_f).astype(jnp.bfloat16)
            value_grad[slot, :, lanes] = (cotangent * out_field).astype(jnp.bfloat16)
    for part in range(per_row):
        lagged = got[pl.ds(2 * slots * per_row + part, groups, stride=pieces), :]
        filter_grad[:, part * LANES : (part + 1) * LANES] = scale * jnp.sum(lagged, axis=0, keepdims=True)


def on_device(kernel, shapes, spaces, scratch=(), aliases=None, out_space=VMEM):
    outs = jax.tree.map(lambda shape: out_space, shapes)
    return pl.pallas_call(
        kernel,
        out_shape=shapes,
        in_specs=spaces,
        out_specs=outs,
        scratch_shapes=scratch,
        input_output_aliases=aliases or {},
        compiler_params=pltpu.CompilerParams(vmem_limit_bytes=LIMIT),
    )


def in_hbm(array):
    return pltpu.with_memory_space_constraint(jnp.asarray(array), pltpu.HBM)


def exchange(rows, axis, count, among=None):
    blocks = rows.reshape(count, 1, rows.size // count)
    return lax.all_to_all(blocks, axis, 0, 0, tiled=True, axis_index_groups=among).reshape(rows.shape)


def local(query, key_in, value, grad_out, filters, skip):
    parts = lax.axis_size("seq")
    chans = lax.axis_size("chan")
    slots, groups, length = query.shape
    total = parts * length
    side = math.isqrt(2 * total)
    pieces = (2 * slots + 1) * length // LANES
    count = parts // COPIES
    packed = jax.ShapeDtypeStruct((parts * pieces, LANES), jnp.float32)
    tables = fourier_tables(side, parts)
    shapes = (
        packed,
        jax.ShapeDtypeStruct((4, *query.shape), query.dtype),
    )
    scratch = [pltpu.VMEM(filters.shape, jnp.float32), pltpu.SemaphoreType.DMA((5,))]
    sent, inputs = on_device(gate_kernel, shapes, [HBM] * 5, scratch)(
        *[in_hbm(array) for array in (query, key_in, value, grad_out, filters)]
    )
    got = exchange(sent, "seq", parts)
    lag_rows = jax.ShapeDtypeStruct((side // 2 // COPIES, LANES), jnp.float32)
    lags = functools.partial(spectral_kernel, side, parts, 2 * slots, lag_product)
    lags = on_device(lags, lag_rows, [VMEM] * 5)(got, *tables)
    moves = [
        (s * chans + k, s * chans + (s // COPIES - k) % chans) for s in range(parts) for k in range(chans)
    ]
    lags = lax.ppermute(lags, ("seq", "chan"), moves)
    packed = jax.ShapeDtypeStruct((count * pieces, LANES), jnp.float32)
    rows = functools.partial(spectral_kernel, side, parts, 2 * slots + 1, filtered)
    held = jax.ShapeDtypeStruct(skip.shape, skip.dtype)
    rows = functools.partial(filter_kernel, rows)
    rows, gains = on_device(rows, (packed, held), [*[VMEM] * 5, HBM], [pltpu.SemaphoreType.DMA])(
        got, *tables, in_hbm(skip)
    )
    sent = on_device(functools.partial(pack_kernel, count), packed, [VMEM] * 2, aliases={0: 0})(rows, lags)
    got = exchange(sent, "seq", count, [list(range(twin, parts, COPIES)) for twin in range(COPIES)])
    grad = jax.ShapeDtypeStruct(query.shape, jnp.bfloat16)
    row = jax.ShapeDtypeStruct((1, length), jnp.float32)
    scale = 1.0 / math.sqrt(slots * chans * total)
    grads = functools.partial(grads_kernel, scale)
    return on_device(grads, (grad, grad, grad, row), [VMEM] * 3)(got, inputs, gains)


def solution(mesh):
    spread = P("chan", None, "seq")
    return jax.shard_map(
        local,
        mesh=mesh,
        in_specs=(spread, spread, spread, spread, P(None, "seq"), P("chan", None)),
        out_specs=(spread, spread, spread, P("chan", "seq")),
        check_vma=False,
    )
```

```python
import functools
import math

import jax
import jax.numpy as jnp
import ml_dtypes
import numpy as np
from jax import lax
from jax.experimental import pallas as pl
from jax.experimental.pallas import tpu as pltpu
from jax.sharding import PartitionSpec as P

LANES = 128
VMEM = pl.BlockSpec(memory_space=pltpu.VMEM)
HBM = pl.BlockSpec(memory_space=pltpu.HBM)
LIMIT = 16 * 1024 * 1024
COPIES = 2
OFFSETS = (12, 4, 5, 15, 7, 11, 8, 9, 0, 1, 3, 2, 10, 6, 14, 13)


def plane_order():
    return sorted(range(len(OFFSETS)), key=OFFSETS.__getitem__)


def block_order():
    return [plane * COPIES + twin for plane in plane_order() for twin in range(COPIES)]


def split_table(table):
    high = table.astype(ml_dtypes.bfloat16)
    low = (table - high.astype(np.float64)).astype(ml_dtypes.bfloat16)
    return high, low


def half_rows(side):
    return -(-(side // 2 + 1) // 8) * 8


def fourier_tables(side, parts):
    used = side // 2 + 1
    rows = half_rows(side)
    per_block = side // 2 // parts
    order = np.arange(side // 2).reshape(parts, per_block)[block_order()].T.reshape(-1)
    coarse = np.arange(used)
    angle = 2.0 * math.pi / side * (coarse[:, None] * order[None, :] % side)
    first = np.zeros((2, rows, side // 2))
    first[0, :used] = np.cos(angle)
    first[1, :used] = -np.sin(angle)
    first = first.reshape(2 * rows, side // 2)
    weight = np.full((used,), 2.0)
    weight[0] = weight[-1] = 1.0
    last = np.zeros((side // 2, 2, rows))
    last[:, 0, :used] = (weight[:, None] * np.cos(angle)).T / side**2
    last[:, 1, :used] = (weight[:, None] * np.sin(angle)).T / side**2
    last = last.reshape(per_block, parts // COPIES, COPIES, 2 * rows)
    last = last.transpose(2, 0, 1, 3).reshape(side // 2, 2 * rows)
    turn = 2.0 * math.pi / side**2 * (coarse[:, None] * np.arange(side)[None, :])
    twist = np.zeros((2, rows, side))
    twist[0, :used] = np.cos(turn)
    twist[1, :used] = -np.sin(turn)
    fine = 2.0 * math.pi / side * (np.arange(side)[:, None] * np.arange(side)[None, :] % side)
    fine_re, fine_im = np.cos(fine), -np.sin(fine)
    fine = np.concatenate([fine_re, fine_im], axis=1)
    twist = np.concatenate([twist[0], twist[1]], axis=1)
    first_high, first_low = split_table(first)
    first = np.concatenate([first_high, first_high, first_low], axis=1)
    blocks = [*split_table(fine), first, *split_table(last), *split_table(twist)]
    wide = max(block.shape[1] for block in blocks)
    stacked = [np.pad(block, ((0, -block.shape[0] % 16), (0, wide - block.shape[1]))) for block in blocks]
    return np.concatenate(stacked, axis=0)


def table_slices(side):
    rows = half_rows(side)
    sizes = ((side, 2 * side),) * 2 + ((2 * rows, 3 * side // 2),) + ((side // 2, 2 * rows),) * 2 + ((rows, 2 * side),) * 2
    starts = np.cumsum([0] + [-(-size[0] // 16) * 16 for size in sizes])
    return [
        (slice(int(start), int(start) + height), slice(0, width))
        for start, (height, width) in zip(starts, sizes)
    ]


def halves(values):
    high = values.astype(jnp.bfloat16)
    low = (values - high.astype(jnp.float32)).astype(jnp.bfloat16)
    return high, low


def matmul(left, right):
    return jnp.dot(left, right, preferred_element_type=jnp.float32)


def xor_rows(values, offset):
    count = values.shape[0]
    row = lax.broadcasted_iota(jnp.int32, values.shape, 0)
    bit = 1
    while bit < count:
        swapped = pltpu.roll(values, bit, 0)
        if 2 * bit < count:
            swapped = jnp.where((row & bit) == 0, pltpu.roll(values, count - bit, 0), swapped)
        values = jnp.where((offset & bit) == 0, values, swapped)
        bit *= 2
    return values


def gate_kernel(
    query, key_in, value, grad_out, filters, tables,
    sent, inputs, tables_held, taps, sems,
):
    slots, groups, length = query.shape
    per_row = length // LANES
    pairs = [(source, inputs.at[place]) for place, source in enumerate((query, key_in, grad_out, value))]
    pairs += [(filters, taps), (tables, tables_held)]
    copies = [pltpu.make_async_copy(*pair, sems.at[place]) for place, pair in enumerate(pairs)]
    for copy in (copies[5], *copies[:5]):
        copy.start()
    chan = lax.axis_index("chan")
    products = []
    for first, second in ((0, 1), (2, 3)):
        copies[first].wait()
        copies[second].wait()
        for slot in range(slots):
            products.append(inputs[first, slot].astype(jnp.float32) * inputs[second, slot].astype(jnp.float32))
    pieces = (len(products) + 1) * per_row
    copies[4].wait()
    for which, rows in enumerate((*products, taps[...])):
        rows = xor_rows(rows, chan)
        for part in range(per_row):
            for twin in range(COPIES):
                place = pl.ds(twin * pieces + which * per_row + part, groups, stride=COPIES * pieces)
                sent[place, :] = rows[:, part * LANES : (part + 1) * LANES]
    for copy in copies[5:]:
        copy.wait()


def spectral_kernel(side, parts, signals, combine, got, tables, sent):
    tables_at = table_slices(side)
    fine_high, fine_low, first = [tables[place] for place in tables_at[:3]]
    twist_high, twist_low = [tables[place].astype(jnp.float32) for place in tables_at[5:]]
    twist = twist_high + twist_low
    turn_re, turn_im = twist[:, :side], twist[:, side:]
    mix_high, mix_low = [
        jnp.concatenate([table, jnp.concatenate([-table[:, side:], table[:, :side]], axis=1)], axis=0)
        for table in (fine_high, fine_low)
    ]
    rows = half_rows(side)
    per_row = side // 2 // parts
    pieces = got.shape[0] // parts
    count = parts // COPIES
    mine = per_row * count
    twin = lax.rem(lax.axis_index("seq"), COPIES)
    last_high, last_low = [
        tables[pl.ds(pl.multiple_of(place.start + twin * mine, 16), mine), lanes] for place, lanes in tables_at[3:5]
    ]

    def one(which):
        return jnp.concatenate(
            [got[pl.ds(which * per_row + part, parts, stride=pieces), :] for part in range(per_row)], axis=0
        )

    def turned(real, imag):
        return real * turn_re - imag * turn_im, real * turn_im + imag * turn_re

    def mixed(pairs):
        out = []
        for pair in pairs:
            stack = jnp.concatenate(pair, axis=1)
            high = stack.astype(jnp.bfloat16).astype(jnp.float32)
            both = matmul(jnp.concatenate([high, stack - high], axis=0).astype(jnp.bfloat16), mix_high)
            values = both[:rows] + (both[rows:] + matmul(high.astype(jnp.bfloat16), mix_low))
            out.append((values[:, :side], values[:, side:]))
        return out

    def coarse(which):
        high, low = halves(one(which))
        values = matmul(first, jnp.concatenate([high, low, high], axis=0))
        return turned(values[:rows], values[rows:])

    spectra = mixed([coarse(which) for which in range(signals)])
    products = [turned(*pair) for pair in mixed(combine(*spectra))]
    high, low = halves(
        jnp.concatenate([jnp.concatenate(parts_of, axis=1) for parts_of in zip(*products)], axis=0)
    )
    tall = jnp.concatenate([last_high, last_low], axis=0)
    both = matmul(tall, high)
    result = both[:mine] + (both[mine:] + matmul(last_high, low))
    spread = sent.shape[0] > mine
    for which in range(len(products)):
        for part in range(per_row):
            piece = result[part * count : (part + 1) * count, which * side : (which + 1) * side]
            if spread:
                sent[pl.ds(which * per_row + part, count, stride=pieces), :] = piece
            else:
                sent[pl.ds(part * count, count), :] = piece


def lag_product(*spectra):
    real = imag = 0.0
    half = len(spectra) // 2
    for (gated_re, gated_im), (signal_re, signal_im) in zip(spectra[:half], spectra[half:]):
        real += gated_re * signal_re + gated_im * signal_im
        imag += gated_im * signal_re - gated_re * signal_im
    return [(real, imag)]


def filtered(*spectra):
    half = len(spectra) // 2
    taps_re, taps_im = spectra[-1]
    conv = [(taps_re * re - taps_im * im, -(taps_re * im + taps_im * re)) for re, im in spectra[:half]]
    corr = [(taps_re * re + taps_im * im, taps_im * re - taps_re * im) for re, im in spectra[half:-1]]
    return conv + corr


def pack_kernel(count, rows, lags, sent):
    per_row = lags.shape[0] // count
    pieces = sent.shape[0] // count
    for part in range(per_row):
        sent[pl.ds(pieces - per_row + part, count, stride=pieces), :] = lags[pl.ds(part * count, count), :]


def filter_kernel(spectral, got, tables, skip, sent, gains, sem):
    copy = pltpu.make_async_copy(skip, gains, sem)
    copy.start()
    spectral(got, tables, sent)
    copy.wait()


def grads_kernel(scale, got, inputs, skip, query_grad, key_grad, value_grad, filter_grad):
    _, slots, groups, length = inputs.shape
    per_row = length // LANES
    pieces = (2 * slots + 1) * per_row
    chan = lax.axis_index("chan")
    shape = (groups, groups)
    diagonal = lax.broadcasted_iota(jnp.int32, shape, 0) == lax.broadcasted_iota(jnp.int32, shape, 1)
    for slot in range(slots):
        gains = jnp.broadcast_to(skip[slot : slot + 1, :], shape)
        gain = jnp.sum(jnp.where(diagonal, gains, 0.0), axis=1, keepdims=True)
        for part in range(per_row):
            lanes = slice(part * LANES, (part + 1) * LANES)
            base = slot * per_row + part
            conv = xor_rows(got[pl.ds(base, groups, stride=pieces), :], chan)
            corr = xor_rows(got[pl.ds(base + slots * per_row, groups, stride=pieces), :], chan)
            query_f, key_f, cotangent, value_f = [
                inputs[place, slot, :, lanes].astype(jnp.float32) for place in range(4)
            ]
            out_field = conv + gain * (query_f * key_f)
            adjoint = corr + gain * (cotangent * value_f)
            query_grad[slot, :, lanes] = (adjoint * key_f).astype(jnp.bfloat16)
            key_grad[slot, :, lanes] = (adjoint * query_f).astype(jnp.bfloat16)
            value_grad[slot, :, lanes] = (cotangent * out_field).astype(jnp.bfloat16)
    for part in range(per_row):
        lagged = got[pl.ds(2 * slots * per_row + part, groups, stride=pieces), :]
        filter_grad[:, part * LANES : (part + 1) * LANES] = scale * jnp.sum(lagged, axis=0, keepdims=True)


def on_device(kernel, shapes, spaces, scratch=(), aliases=None, out_space=VMEM):
    outs = jax.tree.map(lambda shape: out_space, shapes)
    return pl.pallas_call(
        kernel,
        out_shape=shapes,
        in_specs=spaces,
        out_specs=outs,
        scratch_shapes=scratch,
        input_output_aliases=aliases or {},
        compiler_params=pltpu.CompilerParams(vmem_limit_bytes=LIMIT),
    )


def in_hbm(array):
    return pltpu.with_memory_space_constraint(jnp.asarray(array), pltpu.HBM)


def exchange(rows, axis, count, among=None):
    blocks = rows.reshape(count, 1, rows.size // count)
    return lax.all_to_all(blocks, axis, 0, 0, tiled=True, axis_index_groups=among).reshape(rows.shape)


def local(query, key_in, value, grad_out, filters, skip):
    parts = lax.axis_size("seq")
    chans = lax.axis_size("chan")
    slots, groups, length = query.shape
    total = parts * length
    side = math.isqrt(2 * total)
    pieces = (2 * slots + 1) * length // LANES
    count = parts // COPIES
    packed = jax.ShapeDtypeStruct((parts * pieces, LANES), jnp.float32)
    tables = fourier_tables(side, parts)
    shapes = (
        packed,
        jax.ShapeDtypeStruct((4, *query.shape), query.dtype),
        jax.ShapeDtypeStruct(tables.shape, tables.dtype),
    )
    scratch = [pltpu.VMEM(filters.shape, jnp.float32), pltpu.SemaphoreType.DMA((6,))]
    sent, inputs, tables = on_device(gate_kernel, shapes, [HBM] * 6, scratch)(
        *[in_hbm(array) for array in (query, key_in, value, grad_out, filters, tables)]
    )
    got = exchange(sent, "seq", parts, [block_order()])
    lag_rows = jax.ShapeDtypeStruct((side // 2 // COPIES, LANES), jnp.float32)
    lags = functools.partial(spectral_kernel, side, parts, 2 * slots, lag_product)
    lags = on_device(lags, lag_rows, [VMEM] * 2)(got, tables)
    moves = [
        (s * chans + k, s * chans + (OFFSETS[s // COPIES] ^ k)) for s in range(parts) for k in range(chans)
    ]
    lags = lax.ppermute(lags, ("seq", "chan"), moves)
    packed = jax.ShapeDtypeStruct((count * pieces, LANES), jnp.float32)
    rows = functools.partial(spectral_kernel, side, parts, 2 * slots + 1, filtered)
    held = jax.ShapeDtypeStruct(skip.shape, skip.dtype)
    rows = functools.partial(filter_kernel, rows)
    rows, gains = on_device(rows, (packed, held), [VMEM, VMEM, HBM], [pltpu.SemaphoreType.DMA])(
        got, tables, in_hbm(skip)
    )
    sent = on_device(functools.partial(pack_kernel, count), packed, [VMEM] * 2, aliases={0: 0})(rows, lags)
    got = exchange(sent, "seq", count, [block_order()[twin::COPIES] for twin in range(COPIES)])
    grad = jax.ShapeDtypeStruct(query.shape, jnp.bfloat16)
    row = jax.ShapeDtypeStruct((1, length), jnp.float32)
    scale = 1.0 / math.sqrt(slots * chans * total)
    grads = functools.partial(grads_kernel, scale)
    return on_device(grads, (grad, grad, grad, row), [VMEM] * 3)(got, inputs, gains)


def solution(mesh):
    spread = P("chan", None, "seq")
    return jax.shard_map(
        local,
        mesh=mesh,
        in_specs=(spread, spread, spread, spread, P(None, "seq"), P("chan", None)),
        out_specs=(spread, spread, spread, P("chan", "seq")),
        check_vma=False,
    )
```

```python
import functools
import math

import jax
import jax.numpy as jnp
import ml_dtypes
import numpy as np
from jax import lax
from jax.experimental import pallas as pl
from jax.experimental.pallas import tpu as pltpu
from jax.sharding import PartitionSpec as P

LANES = 128
VMEM = pl.BlockSpec(memory_space=pltpu.VMEM)
HBM = pl.BlockSpec(memory_space=pltpu.HBM)
LIMIT = 16 * 1024 * 1024
COPIES = 2
OFFSETS = (12, 4, 5, 15, 7, 11, 8, 9, 0, 1, 3, 2, 10, 6, 14, 13)


def plane_order():
    return sorted(range(len(OFFSETS)), key=OFFSETS.__getitem__)


def block_order():
    return [plane * COPIES + twin for plane in plane_order() for twin in reversed(range(COPIES))]


def split_table(table):
    high = table.astype(ml_dtypes.bfloat16)
    low = (table - high.astype(np.float64)).astype(ml_dtypes.bfloat16)
    return high, low


def half_rows(side):
    return -(-(side // 2 + 1) // 8) * 8


def fourier_tables(side, parts):
    used = side // 2 + 1
    rows = half_rows(side)
    per_block = side // 2 // parts
    order = np.arange(side // 2).reshape(parts, per_block)[block_order()].T.reshape(-1)
    coarse = np.arange(used)
    angle = 2.0 * math.pi / side * (coarse[:, None] * order[None, :] % side)
    first = np.zeros((2, rows, side // 2))
    first[0, :used] = np.cos(angle)
    first[1, :used] = -np.sin(angle)
    first = first.reshape(2 * rows, side // 2)
    weight = np.full((used,), 2.0)
    weight[0] = weight[-1] = 1.0
    last = np.zeros((side // 2, 2, rows))
    last[:, 0, :used] = (weight[:, None] * np.cos(angle)).T / side**2
    last[:, 1, :used] = (weight[:, None] * np.sin(angle)).T / side**2
    last = last.reshape(per_block, parts // COPIES, COPIES, 2 * rows)
    last = last.transpose(2, 0, 1, 3).reshape(side // 2, 2 * rows)
    turn = 2.0 * math.pi / side**2 * (coarse[:, None] * np.arange(side)[None, :])
    twist = np.zeros((2, rows, side))
    twist[0, :used] = np.cos(turn)
    twist[1, :used] = -np.sin(turn)
    fine = 2.0 * math.pi / side * (np.arange(side)[:, None] * np.arange(side)[None, :] % side)
    fine_re, fine_im = np.cos(fine), -np.sin(fine)
    fine = np.concatenate([fine_re, fine_im], axis=1)
    twist = np.concatenate([twist[0], twist[1]], axis=1)
    first_high, first_low = split_table(first)
    first = np.concatenate([first_high, first_high, first_low], axis=1)
    blocks = [*split_table(fine), first, *split_table(last), *split_table(twist)]
    wide = max(block.shape[1] for block in blocks)
    stacked = [np.pad(block, ((0, -block.shape[0] % 16), (0, wide - block.shape[1]))) for block in blocks]
    return np.concatenate(stacked, axis=0)


def table_slices(side):
    rows = half_rows(side)
    sizes = ((side, 2 * side),) * 2 + ((2 * rows, 3 * side // 2),) + ((side // 2, 2 * rows),) * 2 + ((rows, 2 * side),) * 2
    starts = np.cumsum([0] + [-(-size[0] // 16) * 16 for size in sizes])
    return [
        (slice(int(start), int(start) + height), slice(0, width))
        for start, (height, width) in zip(starts, sizes)
    ]


def halves(values):
    high = values.astype(jnp.bfloat16)
    low = (values - high.astype(jnp.float32)).astype(jnp.bfloat16)
    return high, low


def matmul(left, right):
    return jnp.dot(left, right, preferred_element_type=jnp.float32)


def xor_rows(values, offset):
    count = values.shape[0]
    row = lax.broadcasted_iota(jnp.int32, values.shape, 0)
    bit = 1
    while bit < count:
        swapped = pltpu.roll(values, bit, 0)
        if 2 * bit < count:
            swapped = jnp.where((row & bit) == 0, pltpu.roll(values, count - bit, 0), swapped)
        values = jnp.where((offset & bit) == 0, values, swapped)
        bit *= 2
    return values


def gate_kernel(
    query, key_in, value, grad_out, filters, tables,
    sent, inputs, tables_held, taps, sems,
):
    slots, groups, length = query.shape
    per_row = length // LANES
    pairs = [(source, inputs.at[place]) for place, source in enumerate((query, key_in, grad_out, value))]
    pairs += [(filters, taps), (tables, tables_held)]
    copies = [pltpu.make_async_copy(*pair, sems.at[place]) for place, pair in enumerate(pairs)]
    for copy in (copies[5], *copies[:5]):
        copy.start()
    chan = lax.axis_index("chan")
    products = []
    for first, second in ((0, 1), (2, 3)):
        copies[first].wait()
        copies[second].wait()
        for slot in range(slots):
            products.append(inputs[first, slot].astype(jnp.float32) * inputs[second, slot].astype(jnp.float32))
    pieces = (len(products) + 1) * per_row
    copies[4].wait()
    for which, rows in enumerate((*products, taps[...])):
        rows = xor_rows(rows, chan)
        for part in range(per_row):
            for twin in range(COPIES):
                place = pl.ds(twin * pieces + which * per_row + part, groups, stride=COPIES * pieces)
                sent[place, :] = rows[:, part * LANES : (part + 1) * LANES]
    for copy in copies[5:]:
        copy.wait()


def spectral_kernel(side, parts, signals, combine, got, tables, sent):
    tables_at = table_slices(side)
    fine_high, fine_low, first = [tables[place] for place in tables_at[:3]]
    twist_high, twist_low = [tables[place].astype(jnp.float32) for place in tables_at[5:]]
    twist = twist_high + twist_low
    turn_re, turn_im = twist[:, :side], twist[:, side:]
    mix_high, mix_low = [
        jnp.concatenate([table, jnp.concatenate([-table[:, side:], table[:, :side]], axis=1)], axis=0)
        for table in (fine_high, fine_low)
    ]
    rows = half_rows(side)
    per_row = side // 2 // parts
    pieces = got.shape[0] // parts
    count = parts // COPIES
    mine = per_row * count
    twin = COPIES - 1 - lax.rem(lax.axis_index("seq"), COPIES)
    last_high, last_low = [
        tables[pl.ds(pl.multiple_of(place.start + twin * mine, 16), mine), lanes] for place, lanes in tables_at[3:5]
    ]

    def one(which):
        return jnp.concatenate(
            [got[pl.ds(which * per_row + part, parts, stride=pieces), :] for part in range(per_row)], axis=0
        )

    def turned(real, imag):
        return real * turn_re - imag * turn_im, real * turn_im + imag * turn_re

    def mixed(pairs):
        out = []
        for pair in pairs:
            stack = jnp.concatenate(pair, axis=1)
            high = stack.astype(jnp.bfloat16).astype(jnp.float32)
            both = matmul(jnp.concatenate([high, stack - high], axis=0).astype(jnp.bfloat16), mix_high)
            values = both[:rows] + (both[rows:] + matmul(high.astype(jnp.bfloat16), mix_low))
            out.append((values[:, :side], values[:, side:]))
        return out

    def coarse(which):
        high, low = halves(one(which))
        values = matmul(first, jnp.concatenate([high, low, high], axis=0))
        return turned(values[:rows], values[rows:])

    spectra = mixed([coarse(which) for which in range(signals)])
    products = [turned(*pair) for pair in mixed(combine(*spectra))]
    high, low = halves(
        jnp.concatenate([jnp.concatenate(parts_of, axis=1) for parts_of in zip(*products)], axis=0)
    )
    tall = jnp.concatenate([last_high, last_low], axis=0)
    both = matmul(tall, high)
    result = both[:mine] + (both[mine:] + matmul(last_high, low))
    spread = sent.shape[0] > mine
    for which in range(len(products)):
        for part in range(per_row):
            piece = result[part * count : (part + 1) * count, which * side : (which + 1) * side]
            if spread:
                sent[pl.ds(which * per_row + part, count, stride=pieces), :] = piece
            else:
                sent[pl.ds(part * count, count), :] = piece


def lag_product(*spectra):
    real = imag = 0.0
    half = len(spectra) // 2
    for (gated_re, gated_im), (signal_re, signal_im) in zip(spectra[:half], spectra[half:]):
        real += gated_re * signal_re + gated_im * signal_im
        imag += gated_im * signal_re - gated_re * signal_im
    return [(real, imag)]


def filtered(*spectra):
    half = len(spectra) // 2
    taps_re, taps_im = spectra[-1]
    conv = [(taps_re * re - taps_im * im, -(taps_re * im + taps_im * re)) for re, im in spectra[:half]]
    corr = [(taps_re * re + taps_im * im, taps_im * re - taps_re * im) for re, im in spectra[half:-1]]
    return conv + corr


def pack_kernel(count, rows, lags, sent):
    per_row = lags.shape[0] // count
    pieces = sent.shape[0] // count
    for part in range(per_row):
        sent[pl.ds(pieces - per_row + part, count, stride=pieces), :] = lags[pl.ds(part * count, count), :]


def filter_kernel(spectral, got, tables, skip, sent, gains, sem):
    copy = pltpu.make_async_copy(skip, gains, sem)
    copy.start()
    spectral(got, tables, sent)
    copy.wait()


def grads_kernel(scale, got, inputs, skip, query_grad, key_grad, value_grad, filter_grad):
    _, slots, groups, length = inputs.shape
    per_row = length // LANES
    pieces = (2 * slots + 1) * per_row
    chan = lax.axis_index("chan")
    shape = (groups, groups)
    diagonal = lax.broadcasted_iota(jnp.int32, shape, 0) == lax.broadcasted_iota(jnp.int32, shape, 1)
    for slot in range(slots):
        gains = jnp.broadcast_to(skip[slot : slot + 1, :], shape)
        gain = jnp.sum(jnp.where(diagonal, gains, 0.0), axis=1, keepdims=True)
        for part in range(per_row):
            lanes = slice(part * LANES, (part + 1) * LANES)
            base = slot * per_row + part
            conv = xor_rows(got[pl.ds(base, groups, stride=pieces), :], chan)
            corr = xor_rows(got[pl.ds(base + slots * per_row, groups, stride=pieces), :], chan)
            query_f, key_f, cotangent, value_f = [
                inputs[place, slot, :, lanes].astype(jnp.float32) for place in range(4)
            ]
            out_field = conv + gain * (query_f * key_f)
            adjoint = corr + gain * (cotangent * value_f)
            query_grad[slot, :, lanes] = (adjoint * key_f).astype(jnp.bfloat16)
            key_grad[slot, :, lanes] = (adjoint * query_f).astype(jnp.bfloat16)
            value_grad[slot, :, lanes] = (cotangent * out_field).astype(jnp.bfloat16)
    for part in range(per_row):
        lagged = got[pl.ds(2 * slots * per_row + part, groups, stride=pieces), :]
        filter_grad[:, part * LANES : (part + 1) * LANES] = scale * jnp.sum(lagged, axis=0, keepdims=True)


def on_device(kernel, shapes, spaces, scratch=(), aliases=None, out_space=VMEM):
    outs = jax.tree.map(lambda shape: out_space, shapes)
    return pl.pallas_call(
        kernel,
        out_shape=shapes,
        in_specs=spaces,
        out_specs=outs,
        scratch_shapes=scratch,
        input_output_aliases=aliases or {},
        compiler_params=pltpu.CompilerParams(vmem_limit_bytes=LIMIT),
    )


def in_hbm(array):
    return pltpu.with_memory_space_constraint(jnp.asarray(array), pltpu.HBM)


def exchange(rows, axis, count, among=None):
    blocks = rows.reshape(count, 1, rows.size // count)
    return lax.all_to_all(blocks, axis, 0, 0, tiled=True, axis_index_groups=among).reshape(rows.shape)


def local(query, key_in, value, grad_out, filters, skip):
    parts = lax.axis_size("seq")
    chans = lax.axis_size("chan")
    slots, groups, length = query.shape
    total = parts * length
    side = math.isqrt(2 * total)
    pieces = (2 * slots + 1) * length // LANES
    count = parts // COPIES
    packed = jax.ShapeDtypeStruct((parts * pieces, LANES), jnp.float32)
    tables = fourier_tables(side, parts)
    shapes = (
        packed,
        jax.ShapeDtypeStruct((4, *query.shape), query.dtype),
        jax.ShapeDtypeStruct(tables.shape, tables.dtype),
    )
    scratch = [pltpu.VMEM(filters.shape, jnp.float32), pltpu.SemaphoreType.DMA((6,))]
    sent, inputs, tables = on_device(gate_kernel, shapes, [HBM] * 6, scratch)(
        *[in_hbm(array) for array in (query, key_in, value, grad_out, filters, tables)]
    )
    got = exchange(sent, "seq", parts, [block_order()])
    lag_rows = jax.ShapeDtypeStruct((side // 2 // COPIES, LANES), jnp.float32)
    lags = functools.partial(spectral_kernel, side, parts, 2 * slots, lag_product)
    lags = on_device(lags, lag_rows, [VMEM] * 2)(got, tables)
    moves = [
        (s * chans + k, s * chans + (OFFSETS[s // COPIES] ^ k)) for s in range(parts) for k in range(chans)
    ]
    lags = lax.ppermute(lags, ("seq", "chan"), moves)
    packed = jax.ShapeDtypeStruct((count * pieces, LANES), jnp.float32)
    rows = functools.partial(spectral_kernel, side, parts, 2 * slots + 1, filtered)
    held = jax.ShapeDtypeStruct(skip.shape, skip.dtype)
    rows = functools.partial(filter_kernel, rows)
    rows, gains = on_device(rows, (packed, held), [VMEM, VMEM, HBM], [pltpu.SemaphoreType.DMA])(
        got, tables, in_hbm(skip)
    )
    sent = on_device(functools.partial(pack_kernel, count), packed, [VMEM] * 2, aliases={0: 0})(rows, lags)
    got = exchange(sent, "seq", count, [block_order()[twin::COPIES] for twin in range(COPIES)])
    grad = jax.ShapeDtypeStruct(query.shape, jnp.bfloat16)
    row = jax.ShapeDtypeStruct((1, length), jnp.float32)
    scale = 1.0 / math.sqrt(slots * chans * total)
    grads = functools.partial(grads_kernel, scale)
    return on_device(grads, (grad, grad, grad, row), [VMEM] * 3)(got, inputs, gains)


def solution(mesh):
    spread = P("chan", None, "seq")
    return jax.shard_map(
        local,
        mesh=mesh,
        in_specs=(spread, spread, spread, spread, P(None, "seq"), P("chan", None)),
        out_specs=(spread, spread, spread, P("chan", "seq")),
        check_vma=False,
    )
```

```python
import functools
import math

import jax
import jax.numpy as jnp
import ml_dtypes
import numpy as np
from jax import lax
from jax.experimental import pallas as pl
from jax.experimental.pallas import tpu as pltpu
from jax.sharding import PartitionSpec as P

LANES = 128
VMEM = pl.BlockSpec(memory_space=pltpu.VMEM)
HBM = pl.BlockSpec(memory_space=pltpu.HBM)
LIMIT = 16 * 1024 * 1024
COPIES = 2
OFFSETS = (13, 15, 14, 12, 10, 8, 6, 4, 1, 0, 2, 3, 5, 7, 9, 11)


def plane_order():
    return sorted(range(len(OFFSETS)), key=OFFSETS.__getitem__)


def block_order():
    return [plane * COPIES + twin for plane in plane_order() for twin in reversed(range(COPIES))]


def split_table(table):
    high = table.astype(ml_dtypes.bfloat16)
    low = (table - high.astype(np.float64)).astype(ml_dtypes.bfloat16)
    return high, low


def half_rows(side):
    return -(-(side // 2 + 1) // 8) * 8


def fourier_tables(side, parts):
    used = side // 2 + 1
    rows = half_rows(side)
    per_block = side // 2 // parts
    order = np.arange(side // 2).reshape(parts, per_block)[block_order()].T.reshape(-1)
    coarse = np.arange(used)
    angle = 2.0 * math.pi / side * (coarse[:, None] * order[None, :] % side)
    first = np.zeros((2, rows, side // 2))
    first[0, :used] = np.cos(angle)
    first[1, :used] = -np.sin(angle)
    first = first.reshape(2 * rows, side // 2)
    weight = np.full((used,), 2.0)
    weight[0] = weight[-1] = 1.0
    last = np.zeros((side // 2, 2, rows))
    last[:, 0, :used] = (weight[:, None] * np.cos(angle)).T / side**2
    last[:, 1, :used] = (weight[:, None] * np.sin(angle)).T / side**2
    last = last.reshape(per_block, parts // COPIES, COPIES, 2 * rows)
    last = last.transpose(2, 0, 1, 3).reshape(side // 2, 2 * rows)
    turn = 2.0 * math.pi / side**2 * (coarse[:, None] * np.arange(side)[None, :])
    twist = np.zeros((2, rows, side))
    twist[0, :used] = np.cos(turn)
    twist[1, :used] = -np.sin(turn)
    fine = 2.0 * math.pi / side * (np.arange(side)[:, None] * np.arange(side)[None, :] % side)
    fine_re, fine_im = np.cos(fine), -np.sin(fine)
    fine = np.concatenate([fine_re, fine_im], axis=1)
    twist = np.concatenate([twist[0], twist[1]], axis=1)
    first_high, first_low = split_table(first)
    first = np.concatenate([first_high, first_high, first_low], axis=1)
    blocks = [*split_table(fine), first, *split_table(last), *split_table(twist)]
    wide = max(block.shape[1] for block in blocks)
    stacked = [np.pad(block, ((0, -block.shape[0] % 16), (0, wide - block.shape[1]))) for block in blocks]
    return np.concatenate(stacked, axis=0)


def table_slices(side):
    rows = half_rows(side)
    sizes = ((side, 2 * side),) * 2 + ((2 * rows, 3 * side // 2),) + ((side // 2, 2 * rows),) * 2 + ((rows, 2 * side),) * 2
    starts = np.cumsum([0] + [-(-size[0] // 16) * 16 for size in sizes])
    return [
        (slice(int(start), int(start) + height), slice(0, width))
        for start, (height, width) in zip(starts, sizes)
    ]


def halves(values):
    high = values.astype(jnp.bfloat16)
    low = (values - high.astype(jnp.float32)).astype(jnp.bfloat16)
    return high, low


def matmul(left, right):
    return jnp.dot(left, right, preferred_element_type=jnp.float32)


def xor_rows(values, offset):
    count = values.shape[0]
    row = lax.broadcasted_iota(jnp.int32, values.shape, 0)
    bit = 1
    while bit < count:
        swapped = pltpu.roll(values, bit, 0)
        if 2 * bit < count:
            swapped = jnp.where((row & bit) == 0, pltpu.roll(values, count - bit, 0), swapped)
        values = jnp.where((offset & bit) == 0, values, swapped)
        bit *= 2
    return values


def gate_kernel(
    query, key_in, value, grad_out, filters, tables,
    sent, inputs, tables_held, taps, sems,
):
    slots, groups, length = query.shape
    per_row = length // LANES
    pairs = [(source, inputs.at[place]) for place, source in enumerate((query, key_in, grad_out, value))]
    pairs += [(filters, taps), (tables, tables_held)]
    copies = [pltpu.make_async_copy(*pair, sems.at[place]) for place, pair in enumerate(pairs)]
    for copy in (copies[5], *copies[:5]):
        copy.start()
    chan = lax.axis_index("chan")
    products = []
    for first, second in ((0, 1), (2, 3)):
        copies[first].wait()
        copies[second].wait()
        for slot in range(slots):
            products.append(inputs[first, slot].astype(jnp.float32) * inputs[second, slot].astype(jnp.float32))
    pieces = (len(products) + 1) * per_row
    copies[4].wait()
    for which, rows in enumerate((*products, taps[...])):
        rows = xor_rows(rows, chan)
        for part in range(per_row):
            for twin in range(COPIES):
                place = pl.ds(twin * pieces + which * per_row + part, groups, stride=COPIES * pieces)
                sent[place, :] = rows[:, part * LANES : (part + 1) * LANES]
    for copy in copies[5:]:
        copy.wait()


def spectral_kernel(side, parts, signals, combine, got, tables, sent):
    tables_at = table_slices(side)
    fine_high, fine_low, first = [tables[place] for place in tables_at[:3]]
    twist_high, twist_low = [tables[place].astype(jnp.float32) for place in tables_at[5:]]
    twist = twist_high + twist_low
    turn_re, turn_im = twist[:, :side], twist[:, side:]
    mix_high, mix_low = [
        jnp.concatenate([table, jnp.concatenate([-table[:, side:], table[:, :side]], axis=1)], axis=0)
        for table in (fine_high, fine_low)
    ]
    rows = half_rows(side)
    per_row = side // 2 // parts
    pieces = got.shape[0] // parts
    count = parts // COPIES
    mine = per_row * count
    twin = COPIES - 1 - lax.rem(lax.axis_index("seq"), COPIES)
    last_high, last_low = [
        tables[pl.ds(pl.multiple_of(place.start + twin * mine, 16), mine), lanes] for place, lanes in tables_at[3:5]
    ]

    def one(which):
        return jnp.concatenate(
            [got[pl.ds(which * per_row + part, parts, stride=pieces), :] for part in range(per_row)], axis=0
        )

    def turned(real, imag):
        return real * turn_re - imag * turn_im, real * turn_im + imag * turn_re

    def mixed(pairs):
        out = []
        for pair in pairs:
            stack = jnp.concatenate(pair, axis=1)
            high = stack.astype(jnp.bfloat16).astype(jnp.float32)
            both = matmul(jnp.concatenate([high, stack - high], axis=0).astype(jnp.bfloat16), mix_high)
            values = both[:rows] + (both[rows:] + matmul(high.astype(jnp.bfloat16), mix_low))
            out.append((values[:, :side], values[:, side:]))
        return out

    def coarse(which):
        high, low = halves(one(which))
        values = matmul(first, jnp.concatenate([high, low, high], axis=0))
        return turned(values[:rows], values[rows:])

    spectra = mixed([coarse(which) for which in range(signals)])
    products = [turned(*pair) for pair in mixed(combine(*spectra))]
    high, low = halves(
        jnp.concatenate([jnp.concatenate(parts_of, axis=1) for parts_of in zip(*products)], axis=0)
    )
    tall = jnp.concatenate([last_high, last_low], axis=0)
    both = matmul(tall, high)
    result = both[:mine] + (both[mine:] + matmul(last_high, low))
    spread = sent.shape[0] > mine
    for which in range(len(products)):
        for part in range(per_row):
            piece = result[part * count : (part + 1) * count, which * side : (which + 1) * side]
            if spread:
                sent[pl.ds(which * per_row + part, count, stride=pieces), :] = piece
            else:
                sent[pl.ds(part * count, count), :] = piece


def lag_product(*spectra):
    real = imag = 0.0
    half = len(spectra) // 2
    for (gated_re, gated_im), (signal_re, signal_im) in zip(spectra[:half], spectra[half:]):
        real += gated_re * signal_re + gated_im * signal_im
        imag += gated_im * signal_re - gated_re * signal_im
    return [(real, imag)]


def filtered(*spectra):
    half = len(spectra) // 2
    taps_re, taps_im = spectra[-1]
    conv = [(taps_re * re - taps_im * im, -(taps_re * im + taps_im * re)) for re, im in spectra[:half]]
    corr = [(taps_re * re + taps_im * im, taps_im * re - taps_re * im) for re, im in spectra[half:-1]]
    return conv + corr


def pack_kernel(count, rows, lags, sent):
    per_row = lags.shape[0] // count
    pieces = sent.shape[0] // count
    for part in range(per_row):
        sent[pl.ds(pieces - per_row + part, count, stride=pieces), :] = lags[pl.ds(part * count, count), :]


def filter_kernel(spectral, got, tables, skip, sent, gains, sem):
    copy = pltpu.make_async_copy(skip, gains, sem)
    copy.start()
    spectral(got, tables, sent)
    copy.wait()


def grads_kernel(scale, got, inputs, skip, query_grad, key_grad, value_grad, filter_grad):
    _, slots, groups, length = inputs.shape
    per_row = length // LANES
    pieces = (2 * slots + 1) * per_row
    chan = lax.axis_index("chan")
    shape = (groups, groups)
    diagonal = lax.broadcasted_iota(jnp.int32, shape, 0) == lax.broadcasted_iota(jnp.int32, shape, 1)
    for slot in range(slots):
        gains = jnp.broadcast_to(skip[slot : slot + 1, :], shape)
        gain = jnp.sum(jnp.where(diagonal, gains, 0.0), axis=1, keepdims=True)
        for part in range(per_row):
            lanes = slice(part * LANES, (part + 1) * LANES)
            base = slot * per_row + part
            conv = xor_rows(got[pl.ds(base, groups, stride=pieces), :], chan)
            corr = xor_rows(got[pl.ds(base + slots * per_row, groups, stride=pieces), :], chan)
            query_f, key_f, cotangent, value_f = [
                inputs[place, slot, :, lanes].astype(jnp.float32) for place in range(4)
            ]
            out_field = conv + gain * (query_f * key_f)
            adjoint = corr + gain * (cotangent * value_f)
            query_grad[slot, :, lanes] = (adjoint * key_f).astype(jnp.bfloat16)
            key_grad[slot, :, lanes] = (adjoint * query_f).astype(jnp.bfloat16)
            value_grad[slot, :, lanes] = (cotangent * out_field).astype(jnp.bfloat16)
    for part in range(per_row):
        lagged = got[pl.ds(2 * slots * per_row + part, groups, stride=pieces), :]
        filter_grad[:, part * LANES : (part + 1) * LANES] = scale * jnp.sum(lagged, axis=0, keepdims=True)


def on_device(kernel, shapes, spaces, scratch=(), aliases=None, out_space=VMEM):
    outs = jax.tree.map(lambda shape: out_space, shapes)
    return pl.pallas_call(
        kernel,
        out_shape=shapes,
        in_specs=spaces,
        out_specs=outs,
        scratch_shapes=scratch,
        input_output_aliases=aliases or {},
        compiler_params=pltpu.CompilerParams(vmem_limit_bytes=LIMIT),
    )


def in_hbm(array):
    return pltpu.with_memory_space_constraint(jnp.asarray(array), pltpu.HBM)


def exchange(rows, axis, count, among=None):
    blocks = rows.reshape(count, 1, rows.size // count)
    return lax.all_to_all(blocks, axis, 0, 0, tiled=True, axis_index_groups=among).reshape(rows.shape)


def local(query, key_in, value, grad_out, filters, skip):
    parts = lax.axis_size("seq")
    chans = lax.axis_size("chan")
    slots, groups, length = query.shape
    total = parts * length
    side = math.isqrt(2 * total)
    pieces = (2 * slots + 1) * length // LANES
    count = parts // COPIES
    packed = jax.ShapeDtypeStruct((parts * pieces, LANES), jnp.float32)
    tables = fourier_tables(side, parts)
    shapes = (
        packed,
        jax.ShapeDtypeStruct((4, *query.shape), query.dtype),
        jax.ShapeDtypeStruct(tables.shape, tables.dtype),
    )
    scratch = [pltpu.VMEM(filters.shape, jnp.float32), pltpu.SemaphoreType.DMA((6,))]
    sent, inputs, tables = on_device(gate_kernel, shapes, [HBM] * 6, scratch)(
        *[in_hbm(array) for array in (query, key_in, value, grad_out, filters, tables)]
    )
    got = exchange(sent, "seq", parts, [block_order()])
    lag_rows = jax.ShapeDtypeStruct((side // 2 // COPIES, LANES), jnp.float32)
    lags = functools.partial(spectral_kernel, side, parts, 2 * slots, lag_product)
    lags = on_device(lags, lag_rows, [VMEM] * 2)(got, tables)
    moves = [
        (s * chans + k, s * chans + (OFFSETS[s // COPIES] ^ k)) for s in range(parts) for k in range(chans)
    ]
    lags = lax.ppermute(lags, ("seq", "chan"), moves)
    packed = jax.ShapeDtypeStruct((count * pieces, LANES), jnp.float32)
    rows = functools.partial(spectral_kernel, side, parts, 2 * slots + 1, filtered)
    held = jax.ShapeDtypeStruct(skip.shape, skip.dtype)
    rows = functools.partial(filter_kernel, rows)
    rows, gains = on_device(rows, (packed, held), [VMEM, VMEM, HBM], [pltpu.SemaphoreType.DMA])(
        got, tables, in_hbm(skip)
    )
    sent = on_device(functools.partial(pack_kernel, count), packed, [VMEM] * 2, aliases={0: 0})(rows, lags)
    got = exchange(sent, "seq", count, [block_order()[twin::COPIES] for twin in range(COPIES)])
    grad = jax.ShapeDtypeStruct(query.shape, jnp.bfloat16)
    row = jax.ShapeDtypeStruct((1, length), jnp.float32)
    scale = 1.0 / math.sqrt(slots * chans * total)
    grads = functools.partial(grads_kernel, scale)
    return on_device(grads, (grad, grad, grad, row), [VMEM] * 3)(got, inputs, gains)


def solution(mesh):
    spread = P("chan", None, "seq")
    return jax.shard_map(
        local,
        mesh=mesh,
        in_specs=(spread, spread, spread, spread, P(None, "seq"), P("chan", None)),
        out_specs=(spread, spread, spread, P("chan", "seq")),
        check_vma=False,
    )
```
